256 devices in a mesh: row: 4 (over y), col: 16 (over x, z_lo, core), depth: 4 (over z_hi).
Axes of the slice: x: 4, y: 4, z: 8 (z_hi: 4, z_lo: 2; z = z_hi * 2 + z_lo), core: 2. Of those that a mesh axis runs over, the one named last changes fastest.
Arguments:
- coverage: bfloat16 [12288, 16384], P('row', 'col'), may hold values from 0 to 8
- block_mask: int32 [96, 128], P('row', 'col'), may hold values from 0 to 1
- edge_prior: bfloat16 [16384, 512], P('col', 'depth'), may hold values from 0.25 to 4
- test_cost: int32 [12288, 512], P('row', 'depth'), may hold values from 1 to 16
Outputs:
- edge_weights: float32 [16384, 512], P('col', 'depth')
- primal: float32 [12288, 512], P(('row', 'col'), 'depth')
The draws below stay inside these ranges and needn't reach their ends.
All inputs are finite; a program needn't handle non-finite values.
Results may differ from the reference program's by a relative error of at most 0.0003.
Values may be sent and summed in bfloat16 or wider, within the bound.
No kernel may reach another device: no remote copies, remote signals or barrier semaphores. Data moves between devices by JAX's collectives and lax.ppermute only.
A program may use at most 64 MiB of HBM per device.

```python
import math
import jax
import jax.numpy as jnp
from jax import lax

EDGES = 16384
SCEN = 512
BLOCK = 128
ITERS = 2
TESTS = 12288


def draw_coverage(key, part):
    key = jax.random.fold_in(key, 11)
    keys = jax.random.split(key, 3)
    edge_blocks = EDGES // BLOCK
    test_blocks = TESTS // BLOCK
    place = jnp.arange(edge_blocks, dtype=jnp.float32) / edge_blocks
    phase = jax.random.uniform(keys[0], (), jnp.float32)
    rough = jax.random.uniform(keys[1], (edge_blocks,), jnp.float32, -0.35, 0.35)
    wave = jnp.sin(2.0 * math.pi * (place + phase))
    level = jnp.exp(1.2 * wave + rough)
    entry = jax.random.uniform(keys[2], (TESTS, EDGES), jnp.float32, 0.0, 1.0)
    test_scale = jnp.ones((test_blocks,), jnp.float32)
    column_scale = jnp.repeat(level, BLOCK)[None, :]
    row_scale = jnp.repeat(test_scale, BLOCK)[:, None]
    return (entry * column_scale * row_scale).astype(jnp.bfloat16)


def draw_block_mask(key, part):
    key = jax.random.fold_in(key, 23)
    keys = jax.random.split(key, 2)
    edge_blocks = EDGES // BLOCK
    test_blocks = TESTS // BLOCK
    home = jax.random.randint(keys[0], (test_blocks, 1), 0, edge_blocks, dtype=jnp.int32)
    column = jnp.arange(edge_blocks, dtype=jnp.int32)[None, :]
    spacing = jnp.abs(column - home)
    spacing = jnp.minimum(spacing, edge_blocks - spacing)
    nearby = spacing * 8 < edge_blocks
    dice = jax.random.randint(keys[1], (test_blocks, edge_blocks), 0, 100, dtype=jnp.int32)
    return jnp.where(nearby, dice < 85, dice < 5).astype(jnp.int32)


def plant(result, own_key, smallest, top_value):
    extent = result.shape
    spot = [jax.random.randint(jax.random.fold_in(own_key, axis), (), 0, extent[axis]) for axis in range(len(extent))]
    result = result.at[tuple(spot)].set(smallest)
    longest = extent.index(max(extent))
    spot[longest] = (spot[longest] + 1) % extent[longest]
    return result.at[tuple(spot)].set(top_value)


def steps_of(rng, extent, cuts, smallest, top_value):
    gain = 1.0
    for axis_at, parts in cuts:
        draws = jax.random.uniform(jax.random.fold_in(jax.random.fold_in(rng, 6), axis_at), (parts,), jnp.float32, smallest / len(cuts), top_value / len(cuts))
        gain = gain * jnp.repeat(jnp.exp(draws), extent[axis_at] // parts).reshape((-1,) + (1,) * (len(extent) - 1 - axis_at))
    return gain


def setup_inputs(seed: int = 0) -> dict:
    splits = jax.random.split(jax.random.key(seed), 5)
    coverage = draw_coverage(jax.random.fold_in(splits[4], 71), 0)
    block_mask = draw_block_mask(jax.random.fold_in(splits[4], 71), 0)
    edge_prior = jnp.clip(jnp.exp(math.log(4.0) - 2.7725887 * jax.random.uniform(splits[2], (EDGES, SCEN), jnp.float32) ** steps_of(splits[2], (EDGES, SCEN), ((0, 16), (1, 4)), -0.2, 0.2)), 0.25, 4.0).astype(jnp.bfloat16)
    test_cost = plant(jax.random.randint(splits[3], (TESTS, SCEN), 1, 17), jax.random.fold_in(splits[3], 1), 1, 16).astype(jnp.int32)
    return dict(coverage=coverage, block_mask=block_mask, edge_prior=edge_prior, test_cost=test_cost)


def expand(coverage, block_mask):
    test_count, edge_count = coverage.shape
    tiles = coverage.reshape(test_count // BLOCK, BLOCK, edge_count // BLOCK, BLOCK)
    masked = tiles * block_mask.astype(jnp.bfloat16)[:, None, :, None]
    return masked.reshape(test_count, edge_count)


def reference(coverage, block_mask, edge_prior, test_cost):
    coverage_full = expand(coverage, block_mask)
    cost_float = test_cost.astype(jnp.float32)
    current = edge_prior.astype(jnp.float32)
    ratios = jnp.zeros(test_cost.shape, jnp.float32)
    load_mean = jnp.float32(1.0)
    for iteration in range(ITERS):
        low_weights = current.astype(jnp.bfloat16)
        scores = jnp.dot(coverage_full, low_weights, preferred_element_type=jnp.float32)
        ratios = scores / cost_float
        low_ratios = ratios.astype(jnp.bfloat16)
        edge_load = lax.dot_general(coverage_full, low_ratios, (((0,), (0,)), ((), ())), preferred_element_type=jnp.float32)
        load_mean = jnp.sum(edge_load) / (EDGES * SCEN) + 1e-6
        current = current * jnp.exp(-0.25 * edge_load / load_mean)
    primal = TESTS * ratios / load_mean
    return current, primal
```

```python
import functools

import jax
import jax.numpy as jnp
from jax import lax
from jax.experimental import pallas as pl
from jax.experimental.pallas import tpu as pltpu
from jax.sharding import PartitionSpec as P

EDGES = 16384
SCEN = 512
BLOCK = 128
ITERS = 2
TESTS = 12288
CHUNK = 192
PAIR = 2 * CHUNK
HALF = 4 * PAIR
VMEM_LIMIT = 16 * 1024 * 1024
IN_VMEM = pl.BlockSpec(memory_space=pltpu.VMEM)
IN_SMEM = pl.BlockSpec(memory_space=pltpu.SMEM)
ANYWHERE = pl.BlockSpec(memory_space=pl.ANY)
IN_HBM = pl.BlockSpec(memory_space=pltpu.HBM)
f32 = jnp.float32
bf16 = jnp.bfloat16


def call(kernel, out_shape, in_specs, out_specs, flops, scratch=()):
    return pl.pallas_call(
        kernel,
        in_specs=in_specs,
        out_specs=out_specs,
        out_shape=out_shape,
        scratch_shapes=list(scratch),
        compiler_params=pltpu.CompilerParams(vmem_limit_bytes=VMEM_LIMIT),
        cost_estimate=pl.CostEstimate(flops=flops, bytes_accessed=flops // 400, transcendentals=0),
    )


def keep(tile, mask_ref, chunk):
    rows = []
    half = BLOCK // 2
    for j in range(CHUNK // half):
        block_row = (chunk * (CHUNK // half) + j) // 2
        cols = []
        for e in range(tile.shape[1] // BLOCK):
            part = tile[j * half : (j + 1) * half, e * BLOCK : (e + 1) * BLOCK]
            entry = mask_ref[block_row, e].astype(f32)
            cols.append(part * jnp.full(part.shape, entry, f32).astype(bf16))
        rows.append(jnp.concatenate(cols, axis=1))
    return jnp.concatenate(rows, axis=0)


def first_scores_kernel(place_ref, mask_ref, cover_ref, prior_ref, out_ref, kept_ref, weights_ref, sems):
    def chunk(d, z):
        return lax.rem(place_ref[0] + d, 4) * 4 + z * 2 + place_ref[1]

    weights = pltpu.make_async_copy(prior_ref, weights_ref, sems.at[8])
    weights.start()
    copies = []
    for d in range(4):
        for z in range(2):
            spot = d * 2 + z
            rows = pl.ds(pl.multiple_of(chunk(d, z) * CHUNK, CHUNK), CHUNK)
            copy = pltpu.make_async_copy(
                cover_ref.at[rows, :], kept_ref.at[pl.ds(spot * CHUNK, CHUNK), :], sems.at[spot]
            )
            copy.start()
            copies.append(copy)
    weights.wait()
    for d in range(4):
        for z in range(2):
            spot = d * 2 + z
            copies[spot].wait()
            rows = slice(spot * CHUNK, (spot + 1) * CHUNK)
            kept_ref[rows, :] = keep(kept_ref[rows, :], mask_ref, chunk(d, z))
        rows = slice(d * PAIR, (d + 1) * PAIR)
        out_ref[rows, :] = jnp.dot(kept_ref[rows, :], weights_ref[...], preferred_element_type=f32)


def first_scores(cover, mask, prior, place):
    edges, scen = prior.shape
    return call(
        first_scores_kernel,
        [jax.ShapeDtypeStruct((HALF, scen), f32), pltpu.VMEM((HALF, edges), bf16)],
        [IN_SMEM, IN_SMEM, IN_HBM, IN_HBM],
        [IN_VMEM, IN_VMEM],
        2 * HALF * edges * scen,
        [pltpu.VMEM(prior.shape, prior.dtype), pltpu.SemaphoreType.DMA((9,))],
    )(place, mask, in_hbm(cover), in_hbm(prior))


def scores_kernel(kept_ref, weights_ref, out_ref):
    for d in range(4):
        rows = slice(d * PAIR, (d + 1) * PAIR)
        out_ref[rows, :] = jnp.dot(kept_ref[rows, :], weights_ref[...], preferred_element_type=f32)


def later_scores(kept, weights):
    edges, scen = weights.shape
    return call(
        scores_kernel,
        jax.ShapeDtypeStruct((HALF, scen), f32),
        [IN_VMEM, IN_VMEM],
        IN_VMEM,
        2 * HALF * edges * scen,
    )(in_vmem(kept), weights)


def in_vmem(value):
    return pltpu.with_memory_space_constraint(value, pltpu.VMEM)


def in_hbm(value):
    return pltpu.with_memory_space_constraint(value, pltpu.HBM)


def flip_kernel(place_ref, own_ref, other_ref, after_ref, own_out, other_out, sums_ref):
    for half, (kept_ref, out_ref) in enumerate(((own_ref, own_out), (other_ref, other_out))):
        core = lax.rem(place_ref[1] + half, 2)
        for d in range(4):
            x = lax.rem(place_ref[0] + 4 - d, 4)
            tile = kept_ref[pl.ds((4 - d) % 4 * PAIR, PAIR), :]
            out_ref[:, d * PAIR : (d + 1) * PAIR] = tile.T
            ones = jnp.ones((8, tile.shape[1]), bf16)
            sums = lax.dot_general(ones, tile, (((1,), (1,)), ((), ())), preferred_element_type=f32)
            sums_ref[:, pl.ds(pl.multiple_of((core * 4 + x) * PAIR, BLOCK), PAIR)] = sums


def flip(own, other, place, after):
    edges = own.shape[1]
    return call(
        flip_kernel,
        [pltpu.VMEM((edges, HALF), bf16), pltpu.VMEM((edges, HALF), bf16), jax.ShapeDtypeStruct((8, 2 * HALF), f32)],
        [IN_SMEM, IN_VMEM, IN_VMEM, ANYWHERE],
        [IN_VMEM, IN_VMEM, IN_VMEM],
        16 * HALF * edges * 128,
    )(place, in_vmem(own), in_vmem(other), after)


def column_sums(low):
    return jnp.dot(jnp.ones((8, low.shape[0]), bf16), low, preferred_element_type=f32)


def half_loads_kernel(flipped_ref, low0, low1, low2, low3, load_ref, size_ref):
    load = jnp.zeros(load_ref.shape, f32)
    size = jnp.zeros(size_ref.shape, f32)
    for d, low in enumerate((low0, low1, low2, low3)):
        load += jnp.dot(flipped_ref[:, d * PAIR : (d + 1) * PAIR], low[...], preferred_element_type=f32)
        size += column_sums(low[...])
    load_ref[...] = load
    size_ref[...] = size


def whole_loads_kernel(flipped_ref, low0, low1, low2, low3, load_in, size_in, wire_ref):
    load = load_in[...]
    size = size_in[...]
    for d, low in enumerate((low0, low1, low2, low3)):
        load += jnp.dot(flipped_ref[:, d * PAIR : (d + 1) * PAIR], low[...], preferred_element_type=f32)
        size += column_sums(low[...])
    power = jnp.floor(jnp.log2(jnp.maximum(size, 1e-30)))
    edges = load.shape[0]
    wire_ref[:edges, :] = load * jnp.exp2(11.0 - power[:1, :])
    wire_ref[edges:, :] = jnp.concatenate([power, power], axis=0)


def half_loads(flipped, lows):
    edges, scen = flipped.shape[0], lows[0].shape[1]
    return call(
        half_loads_kernel,
        [jax.ShapeDtypeStruct((edges, scen), f32), jax.ShapeDtypeStruct((8, scen), f32)],
        [IN_VMEM] * 5,
        [IN_VMEM, IN_VMEM],
        2 * HALF * edges * scen,
    )(in_vmem(flipped), *lows)


def whole_loads(flipped, lows, load, size):
    edges, scen = load.shape
    wire = call(
        whole_loads_kernel,
        jax.ShapeDtypeStruct((edges + 16, scen), f32),
        [IN_VMEM] * 7,
        IN_VMEM,
        2 * HALF * edges * scen,
    )(in_vmem(flipped), *lows, load, size)
    return wire.astype(jnp.float16)


def from_wire(wire):
    wire = wire.astype(f32)
    edges = wire.shape[0] - 16
    return wire[:edges] * jnp.exp2(wire[edges : edges + 1] - 11.0)


def total_kernel(place_ref, sums_ref, *refs):
    *lows, after_ref, out_ref = refs
    total = jnp.zeros(out_ref.shape, f32)
    first = lax.broadcasted_iota(jnp.int32, (8, PAIR), 0) == 0
    for n, low in enumerate(lows):
        core = lax.rem(place_ref[1] + n // 4, 2)
        x = lax.rem(place_ref[0] + 4 - n % 4, 4)
        left = sums_ref[:, pl.ds(pl.multiple_of((core * 4 + x) * PAIR, BLOCK), PAIR)]
        left = jnp.where(first, left, 0.0)
        for _ in range(3):
            part = left.astype(bf16)
            left = left - part.astype(f32)
            total += jnp.dot(part, low[...], preferred_element_type=f32)
    out_ref[...] = jnp.full(out_ref.shape, jnp.sum(total), f32)


def total_load(sums, lows, place, after):
    return call(
        total_kernel,
        jax.ShapeDtypeStruct((8, lows[0].shape[1]), f32),
        [IN_SMEM] + [IN_VMEM] * 9 + [ANYWHERE],
        IN_VMEM,
        10**8,
    )(place, sums, *lows, after)


def ring(n, d, stride=1):
    return [(i, (i + d * stride) % n) for i in range(n)]


def swap(bit):
    return [(i, i ^ bit) for i in range(16)]


def shifts(value, axis):
    return [lax.ppermute(value, axis, ring(4, d)) for d in (1, 2, 3)]


def sum_ring(value, axis):
    one, two, three = shifts(value, axis)
    return (value + two) + (one + three)


def body(coverage, block_mask, edge_prior, test_cost):
    at = lax.axis_index("col")
    x, z, core = at // 4, (at // 2) % 2, at % 2
    place = jnp.stack([x, core]).astype(jnp.int32)
    other = jnp.stack([x, 1 - core]).astype(jnp.int32)
    costs = test_cost.reshape(4, 2, 2, CHUNK, test_cost.shape[1])
    cost = lax.dynamic_slice(costs, (x, 0, core, 0, 0), (1, 2, 1, CHUNK, costs.shape[-1]))
    cost = cost.reshape(PAIR, costs.shape[-1]).astype(f32)

    current = edge_prior.astype(f32)
    low_weights = edge_prior
    for iteration in range(ITERS):
        wire = bf16 if iteration == 0 else f32
        with jax.named_scope("scores"):
            if iteration == 0:
                away, kept_away = first_scores(coverage, block_mask, edge_prior, other)
                here, kept_here = first_scores(coverage, block_mask, edge_prior, place)
            else:
                away = later_scores(kept_away, low_weights)
                here = later_scores(kept_here, low_weights)
            here = here + lax.ppermute(away, "col", swap(1))
            here = here.reshape(4, PAIR, -1)
        with jax.named_scope("sum_x"):
            parts = [here[0]] + [
                lax.ppermute(here[d].astype(wire), "col", ring(16, d, 4)).astype(f32) for d in (1, 2, 3)
            ]
            scores = (parts[0] + parts[2]) + (parts[1] + parts[3])
        if iteration == 0:
            with jax.named_scope("flip"):
                flipped_here, flipped_away, sums = flip(kept_here, kept_away, place, scores)
        with jax.named_scope("sum_z"):
            scores = scores + lax.ppermute(scores.astype(wire), "col", swap(2)).astype(f32)
            ratios = scores / cost
            low_ratios = ratios.astype(bf16)
        if iteration == 0:
            with jax.named_scope("row_sums"):
                sums = sums + lax.ppermute(sums, "col", swap(1))
                sums = sums + lax.ppermute(sums, "col", swap(2))
                one, two, three = (lax.ppermute(sums, "col", ring(16, d, 4)) for d in (1, 2, 3))
                sums = (sums + two) + (one + three)
        with jax.named_scope("gather"):
            lows = [low_ratios] + [lax.ppermute(low_ratios, "col", ring(16, d, 4)) for d in (1, 2, 3)]
            away_lows = [lax.ppermute(low, "col", swap(1)) for low in lows]
        with jax.named_scope("loads"):
            load, size = half_loads(flipped_here, lows)
            load = whole_loads(flipped_away, away_lows, load, size)
        with jax.named_scope("mean"):
            after = lax.ppermute(load[-16:], "col", swap(1)).astype(f32)
            total = total_load(sums, lows + away_lows, place, after)
            total = sum_ring(sum_ring(total, "depth"), "row")
            load_mean = total[:1, :1] / (EDGES * SCEN) + 1e-06
        with jax.named_scope("sum_y"):
            loads = [load] + shifts(load, "row")
            zero, one, two, three = map(from_wire, loads)
            edge_load = (zero + two) + (one + three)
        with jax.named_scope("update"):
            current = current * jnp.exp(-0.25 * edge_load / load_mean)
            low_weights = current.astype(bf16)
    own = lax.dynamic_slice_in_dim(ratios, z * CHUNK, CHUNK, 0)
    primal = TESTS * own / load_mean
    return (current, primal)


def solution(mesh):
    placed = (P("row", "col"), P("row", "col"), P("col", "depth"), P("row", "depth"))
    return jax.shard_map(
        body,
        mesh=mesh,
        in_specs=placed,
        out_specs=(P("col", "depth"), P(("row", "col"), "depth")),
        check_vma=False,
    )
```

```python
import functools

import jax
import jax.numpy as jnp
from jax import lax
from jax.experimental import pallas as pl
from jax.experimental.pallas import tpu as pltpu
from jax.sharding import PartitionSpec as P

EDGES = 16384
SCEN = 512
BLOCK = 128
ITERS = 2
TESTS = 12288
CHUNK = 192
PAIR = 2 * CHUNK
HALF = 4 * PAIR
WITH_SUMS = PAIR + 8
GATHERED = PAIR + 32
VMEM_LIMIT = 16 * 1024 * 1024
IN_VMEM = pl.BlockSpec(memory_space=pltpu.VMEM)
IN_SMEM = pl.BlockSpec(memory_space=pltpu.SMEM)
ANYWHERE = pl.BlockSpec(memory_space=pl.ANY)
IN_HBM = pl.BlockSpec(memory_space=pltpu.HBM)
f32 = jnp.float32
bf16 = jnp.bfloat16


def call(kernel, out_shape, in_specs, out_specs, flops, scratch=()):
    return pl.pallas_call(
        kernel,
        in_specs=in_specs,
        out_specs=out_specs,
        out_shape=out_shape,
        scratch_shapes=list(scratch),
        compiler_params=pltpu.CompilerParams(vmem_limit_bytes=VMEM_LIMIT),
        cost_estimate=pl.CostEstimate(flops=flops, bytes_accessed=flops // 400, transcendentals=0),
    )


def in_vmem(value):
    return pltpu.with_memory_space_constraint(value, pltpu.VMEM)


def in_hbm(value):
    return pltpu.with_memory_space_constraint(value, pltpu.HBM)


def first_scores_kernel(place_ref, mask_ref, cover_ref, prior_ref, out_ref, kept_ref, weights_ref, tiles_ref, rows_ref, sems):
    def chunk(d, z):
        return lax.rem(place_ref[0] + d, 4) * 4 + z * 2 + place_ref[1]

    tiles = pltpu.make_async_copy(mask_ref, tiles_ref, sems.at[9])
    tiles.start()
    copies = []
    for d in range(4):
        for z in range(2):
            spot = d * 2 + z
            rows = pl.ds(pl.multiple_of(chunk(d, z) * CHUNK, CHUNK), CHUNK)
            copy = pltpu.make_async_copy(
                cover_ref.at[rows, :], kept_ref.at[pl.ds(spot * CHUNK, CHUNK), :], sems.at[spot]
            )
            copy.start()
            copies.append(copy)
    weights = pltpu.make_async_copy(prior_ref, weights_ref, sems.at[8])
    weights.start()
    edges = cover_ref.shape[1]
    tiles.wait()
    column = lax.broadcasted_iota(jnp.int32, (tiles_ref.shape[1], edges), 1) // BLOCK
    spread = column == lax.broadcasted_iota(jnp.int32, column.shape, 0)
    rows_ref[...] = jnp.dot(
        tiles_ref[...].astype(f32), spread.astype(f32), preferred_element_type=f32
    )
    weights.wait()
    ones = jnp.ones((8, edges), bf16)
    half = BLOCK // 2
    for d in range(4):
        for z in range(2):
            spot = d * 2 + z
            copies[spot].wait()
            for j in range(CHUNK // half):
                block_row = (chunk(d, z) * (CHUNK // half) + j) // 2
                entry = jnp.broadcast_to(rows_ref[pl.ds(block_row, 1), :], (16, edges)).astype(bf16)
                for k in range(half // 16):
                    at = spot * CHUNK + j * half + k * 16
                    kept_ref[at : at + 16, :] = kept_ref[at : at + 16, :] * entry
        kept = kept_ref[d * PAIR : (d + 1) * PAIR, :]
        at = d * WITH_SUMS
        out_ref[at : at + PAIR, :] = jnp.dot(kept, weights_ref[...], preferred_element_type=f32)
        sums = lax.dot_general(ones, kept, (((1,), (1,)), ((), ())), preferred_element_type=f32)
        out_ref[at + PAIR : at + WITH_SUMS, :] = jnp.concatenate(
            [sums[:1, j * BLOCK : (j + 1) * BLOCK] for j in range(3)] + [jnp.zeros((5, BLOCK), f32)], axis=0
        )


def first_scores(cover, mask, prior, place):
    edges, scen = prior.shape
    return call(
        first_scores_kernel,
        [jax.ShapeDtypeStruct((4 * WITH_SUMS, scen), f32), pltpu.VMEM((HALF, edges), bf16)],
        [IN_SMEM, IN_HBM, IN_HBM, IN_HBM],
        [IN_VMEM, IN_VMEM],
        2 * HALF * edges * scen,
        [
            pltpu.VMEM(prior.shape, prior.dtype),
            pltpu.VMEM(mask.shape, mask.dtype),
            pltpu.VMEM((mask.shape[0], edges), f32),
            pltpu.SemaphoreType.DMA((10,)),
        ],
    )(place, in_hbm(mask), in_hbm(cover), in_hbm(prior))


def scores_kernel(kept_ref, weights_ref, out_ref):
    for d in range(4):
        rows = slice(d * PAIR, (d + 1) * PAIR)
        out_ref[rows, :] = jnp.dot(kept_ref[rows, :], weights_ref[...], preferred_element_type=f32)


def later_scores(kept, weights):
    edges, scen = weights.shape
    return call(
        scores_kernel,
        jax.ShapeDtypeStruct((HALF, scen), f32),
        [IN_VMEM, IN_VMEM],
        IN_VMEM,
        2 * HALF * edges * scen,
    )(in_vmem(kept), weights)


def flip_kernel(own_ref, other_ref, after_ref, own_out, other_out):
    for kept_ref, out_ref in ((own_ref, own_out), (other_ref, other_out)):
        for d in range(4):
            tile = kept_ref[pl.ds((4 - d) % 4 * PAIR, PAIR), :]
            out_ref[:, d * PAIR : (d + 1) * PAIR] = tile.T


def flip(own, other, after):
    edges = own.shape[1]
    return call(
        flip_kernel,
        [pltpu.VMEM((edges, HALF), bf16), pltpu.VMEM((edges, HALF), bf16)],
        [IN_VMEM, IN_VMEM, ANYWHERE],
        [IN_VMEM, IN_VMEM],
        16 * HALF * edges * 128,
    )(in_vmem(own), in_vmem(other), after)


def column_sums(low):
    return jnp.dot(jnp.ones((8, low.shape[0]), bf16), low, preferred_element_type=f32)


def add_loads(flipped_ref, low_ref, load, size):
    stride = low_ref.shape[0] // 4
    for d in range(4):
        low = low_ref[d * stride : d * stride + PAIR, :]
        load += jnp.dot(flipped_ref[:, d * PAIR : (d + 1) * PAIR], low, preferred_element_type=f32)
        size += column_sums(low)
    return load, size


def half_loads_kernel(flipped_ref, low_ref, load_ref, size_ref):
    load, size = add_loads(flipped_ref, low_ref, jnp.zeros(load_ref.shape, f32), jnp.zeros(size_ref.shape, f32))
    load_ref[...] = load
    size_ref[...] = size


def whole_loads_kernel(flipped_ref, low_ref, load_in, size_in, load_ref, power_ref):
    load, size = add_loads(flipped_ref, low_ref, load_in[...], size_in[...])
    power = jnp.floor(jnp.log2(jnp.maximum(size, 1e-30)))
    load_ref[...] = load * jnp.exp2(11.0 - power[:1, :])
    power_ref[...] = power


def loads(kernel, flipped, low, *so_far):
    edges, scen = flipped.shape[0], low.shape[1]
    return call(
        kernel,
        [jax.ShapeDtypeStruct((edges, scen), f32), jax.ShapeDtypeStruct((8, scen), f32)],
        [IN_VMEM] * (2 + len(so_far)),
        [IN_VMEM, IN_VMEM],
        2 * HALF * edges * scen,
    )(in_vmem(flipped), low, *so_far)


def total_kernel(sums_own, sums_away, low_own, low_away, out_ref):
    totals = [jnp.zeros((32, BLOCK), f32) for _ in range(3)]
    stride = low_own.shape[0] // 4
    for sums_ref, low_ref in ((sums_own, low_own), (sums_away, low_away)):
        for d in range(4):
            sums = sums_ref[d * GATHERED + PAIR : (d + 1) * GATHERED, :]
            for j in range(3):
                low = low_ref[d * stride + j * BLOCK : d * stride + (j + 1) * BLOCK, :]
                totals[j] += jnp.dot(sums, low, preferred_element_type=f32)
    row = lax.broadcasted_iota(jnp.int32, (32, BLOCK), 0)
    total = jnp.zeros((32, BLOCK), f32)
    for j in range(3):
        total += jnp.where(row % 8 == j, totals[j], 0.0)
    out_ref[...] = jnp.full(out_ref.shape, jnp.sum(total), f32)


def total_load(sums_own, sums_away, low_own, low_away):
    return call(
        total_kernel,
        jax.ShapeDtypeStruct((8, low_own.shape[1]), f32),
        [IN_VMEM] * 4,
        IN_VMEM,
        10**8,
    )(sums_own, sums_away, low_own, low_away)


def bf16_parts(sums):
    parts = []
    left = sums
    for _ in range(3):
        part = lax.reduce_precision(left, 8, 7)
        left = left - part
        parts.append(part)
    return parts + [jnp.zeros_like(sums)]


def pack_sums(value):
    return jnp.concatenate([value[:PAIR]] + bf16_parts(value[PAIR:]), axis=0).astype(bf16)


def unpack_sums(value):
    value = value.astype(f32)
    sums = value[PAIR : PAIR + 8] + value[PAIR + 8 : PAIR + 16] + value[PAIR + 16 : PAIR + 24]
    return jnp.concatenate([value[:PAIR], sums], axis=0)


def pack_int16(value):
    top = jnp.max(value, axis=0, keepdims=True)
    power = jnp.ceil(jnp.log2(jnp.maximum(top, 1e-30)))
    code = jnp.round(value * jnp.exp2(16.0 - power)) - 32768.0
    code = jnp.clip(code, -32768.0, 32767.0)
    tile = jnp.broadcast_to(power, (16, value.shape[1]))
    return jnp.concatenate([code, tile], axis=0).astype(jnp.int32).astype(jnp.int16)


def unpack_int16(value):
    value = value.astype(jnp.int32).astype(f32)
    return (value[:-16] + 32768.0) * jnp.exp2(value[-16:-15] - 16.0)


def pack_load(load, power, total):
    scale = jnp.floor(jnp.log2(jnp.maximum(total, 1e-30)))
    total = total * jnp.exp2(-scale)
    high = lax.reduce_precision(total, 5, 10)
    wire = jnp.concatenate([load, power, scale, high, (total - high) * 1024.0], axis=0)
    return lax.reduce_precision(wire, 5, 10)


def unpack_load(wire):
    wire = wire.astype(f32)
    power, scale, high, low = (wire[at : at + 1] for at in range(wire.shape[0] - 32, wire.shape[0], 8))
    return wire[:-32] * jnp.exp2(power - 11.0), (high + low * (1.0 / 1024.0)) * jnp.exp2(scale)


def ring(n, d, stride=1):
    return [(i, (i + d * stride) % n) for i in range(n)]


def swap(bit):
    return [(i, i ^ bit) for i in range(16)]


def shifts(value, axis):
    return [lax.ppermute(value, axis, ring(4, d)) for d in (1, 2, 3)]


def sum_four(parts):
    zero, one, two, three = parts
    return (zero + two) + (one + three)


def body(coverage, block_mask, edge_prior, test_cost):
    at = lax.axis_index("col")
    x, z, core = at // 4, (at // 2) % 2, at % 2
    place = jnp.stack([x, core]).astype(jnp.int32)
    other = jnp.stack([x, 1 - core]).astype(jnp.int32)
    costs = test_cost.reshape(4, 2, 2, CHUNK, test_cost.shape[1])
    cost = lax.dynamic_slice(costs, (x, 0, core, 0, 0), (1, 2, 1, CHUNK, costs.shape[-1]))
    cost = cost.reshape(PAIR, costs.shape[-1]).astype(f32)

    current = edge_prior.astype(f32)
    low_weights = edge_prior
    for iteration in range(ITERS):
        first = iteration == 0
        pack, unpack = (pack_sums, unpack_sums) if first else (pack_int16, unpack_int16)
        with jax.named_scope("scores"):
            if first:
                away, kept_away = first_scores(coverage, block_mask, edge_prior, other)
                here, kept_here = first_scores(coverage, block_mask, edge_prior, place)
            else:
                away = later_scores(kept_away, low_weights)
                here = later_scores(kept_here, low_weights)
            here = here + lax.ppermute(away, "col", swap(1))
            here = here.reshape(4, -1, here.shape[-1])
        with jax.named_scope("sum_x"):
            parts = [unpack(lax.ppermute(pack(here[d]), "col", ring(16, d, 4))) for d in (1, 2, 3)]
            scores = sum_four([here[0]] + parts)
        if first:
            with jax.named_scope("flip"):
                flipped_here, flipped_away = flip(kept_here, kept_away, scores)
        with jax.named_scope("sum_z"):
            scores = scores + unpack(lax.ppermute(pack(scores), "col", swap(2)))
            ratios = scores[:PAIR] / cost
            low_ratios = ratios.astype(bf16)
            if first:
                sums = [part.astype(bf16) for part in bf16_parts(scores[PAIR:])]
                low_ratios = jnp.concatenate([low_ratios] + sums, axis=0)
        with jax.named_scope("gather"):
            lows = [low_ratios] + [lax.ppermute(low_ratios, "col", ring(16, d, 4)) for d in (1, 2, 3)]
            low_here = jnp.concatenate(lows, axis=0)
            low_away = lax.ppermute(low_here, "col", swap(1))
            if first:
                sums_here, sums_away = low_here, low_away
        with jax.named_scope("total"):
            total = total_load(sums_here, sums_away, low_here, low_away)
            total = sum_four([total] + shifts(total, "depth"))
        with jax.named_scope("loads"):
            half, size = loads(half_loads_kernel, flipped_here, low_here)
            load, power = loads(whole_loads_kernel, flipped_away, low_away, half, size)
        with jax.named_scope("sum_y"):
            wire = pack_load(load, power, total)
            pairs = [unpack_load(part) for part in [wire] + shifts(wire.astype(jnp.float16), "row")]
            edge_load = sum_four([pair[0] for pair in pairs])
            load_mean = sum_four([pair[1] for pair in pairs]) / (EDGES * SCEN) + 1e-06
        with jax.named_scope("update"):
            current = current * jnp.exp(-0.25 * edge_load / load_mean)
            low_weights = current.astype(bf16)
    own = lax.dynamic_slice_in_dim(ratios, z * CHUNK, CHUNK, 0)
    primal = TESTS * own / load_mean
    return (current, primal)


def solution(mesh):
    placed = (P("row", "col"), P("row", "col"), P("col", "depth"), P("row", "depth"))
    return jax.shard_map(
        body,
        mesh=mesh,
        in_specs=placed,
        out_specs=(P("col", "depth"), P(("row", "col"), "depth")),
        check_vma=False,
    )
```

```python
import functools

import jax
import jax.numpy as jnp
from jax import lax
from jax.experimental import pallas as pl
from jax.experimental.pallas import tpu as pltpu
from jax.sharding import PartitionSpec as P

EDGES = 16384
SCEN = 512
BLOCK = 128
ITERS = 2
TESTS = 12288
CHUNK = 192
PAIR = 2 * CHUNK
HALF = 4 * PAIR
WITH_SUMS = PAIR + 8
GATHERED = PAIR + 32
VMEM_LIMIT = 16 * 1024 * 1024
IN_VMEM = pl.BlockSpec(memory_space=pltpu.VMEM)
IN_SMEM = pl.BlockSpec(memory_space=pltpu.SMEM)
ANYWHERE = pl.BlockSpec(memory_space=pl.ANY)
IN_HBM = pl.BlockSpec(memory_space=pltpu.HBM)
f32 = jnp.float32
bf16 = jnp.bfloat16


def call(kernel, out_shape, in_specs, out_specs, flops, scratch=()):
    return pl.pallas_call(
        kernel,
        in_specs=in_specs,
        out_specs=out_specs,
        out_shape=out_shape,
        scratch_shapes=list(scratch),
        compiler_params=pltpu.CompilerParams(vmem_limit_bytes=VMEM_LIMIT),
        cost_estimate=pl.CostEstimate(flops=flops, bytes_accessed=flops // 400, transcendentals=0),
    )


def in_vmem(value):
    return pltpu.with_memory_space_constraint(value, pltpu.VMEM)


def in_hbm(value):
    return pltpu.with_memory_space_constraint(value, pltpu.HBM)


def half_scores(kept_ref, weights, rows_ref, place_ref, core, out_ref, raw_ref=None, wait=None):
    edges = kept_ref.shape[1]
    half = BLOCK // 2
    ones = jnp.ones((8, edges), bf16)
    for d in range(4):
        for z in range(2):
            spot = d * 2 + z
            if wait is not None:
                wait(spot)
            chunk = lax.rem(place_ref[0] + d, 4) * 4 + z * 2 + core
            for j in range(CHUNK // half):
                block_row = (chunk * (CHUNK // half) + j) // 2
                entry = jnp.broadcast_to(rows_ref[pl.ds(block_row, 1), :], (16, edges)).astype(bf16)
                for k in range(half // 16):
                    at = spot * CHUNK + j * half + k * 16
                    source = kept_ref if raw_ref is None else raw_ref
                    kept_ref[at : at + 16, :] = source[at : at + 16, :] * entry
        kept = kept_ref[d * PAIR : (d + 1) * PAIR, :]
        at = d * WITH_SUMS
        out_ref[at : at + PAIR, :] = jnp.dot(kept, weights, preferred_element_type=f32)
        sums = lax.dot_general(ones, kept, (((1,), (1,)), ((), ())), preferred_element_type=f32)
        out_ref[at + PAIR : at + WITH_SUMS, :] = jnp.concatenate(
            [sums[:1, j * BLOCK : (j + 1) * BLOCK] for j in range(3)] + [jnp.zeros((5, BLOCK), f32)], axis=0
        )


def first_scores_kernel(place_ref, mask_ref, cover_ref, prior_ref, out_ref, kept_ref, raw_ref, weights_ref, rows_ref, tiles_ref, sems):
    tiles = pltpu.make_async_copy(mask_ref, tiles_ref, sems.at[16])
    tiles.start()
    copies = []
    for half, held_ref in enumerate((kept_ref, raw_ref)):
        core = place_ref[1] if half else 1 - place_ref[1]
        for spot in range(8):
            chunk = lax.rem(place_ref[0] + spot // 2, 4) * 4 + spot % 2 * 2 + core
            rows = pl.ds(pl.multiple_of(chunk * CHUNK, CHUNK), CHUNK)
            copy = pltpu.make_async_copy(
                cover_ref.at[rows, :], held_ref.at[pl.ds(spot * CHUNK, CHUNK), :], sems.at[half * 8 + spot]
            )
            copy.start()
            copies.append(copy)
        if half == 0:
            weights = pltpu.make_async_copy(prior_ref, weights_ref, sems.at[17])
            weights.start()
    edges = cover_ref.shape[1]
    tiles.wait()
    column = lax.broadcasted_iota(jnp.int32, (tiles_ref.shape[0], edges), 1) // BLOCK
    spread = column == lax.broadcasted_iota(jnp.int32, column.shape, 0)
    rows_ref[...] = lax.dot_general(
        tiles_ref[...].astype(f32), spread.astype(f32), (((0,), (0,)), ((), ())), preferred_element_type=f32
    )
    weights.wait()
    half_scores(
        kept_ref, weights_ref[...], rows_ref, place_ref, 1 - place_ref[1], out_ref, wait=lambda spot: copies[spot].wait()
    )
    for copy in copies[8:]:
        copy.wait()


def own_scores_kernel(place_ref, raw_ref, weights_ref, rows_ref, out_ref, kept_ref):
    half_scores(kept_ref, weights_ref[...], rows_ref, place_ref, place_ref[1], out_ref, raw_ref=raw_ref)


def first_scores(cover, mask, prior, place):
    edges, scen = prior.shape
    tests = BLOCK * mask.shape[0]
    away, kept_away, raw, weights, rows = call(
        first_scores_kernel,
        [
            pltpu.VMEM((4 * WITH_SUMS, scen), f32),
            pltpu.VMEM((HALF, edges), bf16),
            pltpu.VMEM((HALF, edges), bf16),
            pltpu.VMEM(prior.shape, bf16),
            pltpu.VMEM((tests // BLOCK, edges), f32),
        ],
        [IN_SMEM, IN_HBM, IN_HBM, IN_HBM],
        [IN_VMEM] * 5,
        2 * HALF * edges * scen,
        [pltpu.VMEM(mask.shape[::-1], mask.dtype), pltpu.SemaphoreType.DMA((18,))],
    )(place, in_hbm(mask.T), in_hbm(cover), in_hbm(prior))
    here, kept_here = call(
        own_scores_kernel,
        [pltpu.VMEM((4 * WITH_SUMS, scen), f32), pltpu.VMEM((HALF, edges), bf16)],
        [IN_SMEM] + [IN_VMEM] * 3,
        [IN_VMEM] * 2,
        2 * HALF * edges * scen,
    )(place, in_vmem(raw), in_vmem(weights), in_vmem(rows))
    return away, kept_away, here, kept_here


def scores_kernel(kept_ref, weights_ref, out_ref):
    for d in range(4):
        rows = slice(d * PAIR, (d + 1) * PAIR)
        out_ref[rows, :] = jnp.dot(kept_ref[rows, :], weights_ref[...], preferred_element_type=f32)


def later_scores(kept, weights):
    edges, scen = weights.shape
    return call(
        scores_kernel,
        pltpu.VMEM((HALF, scen), f32),
        [IN_VMEM, IN_VMEM],
        IN_VMEM,
        2 * HALF * edges * scen,
    )(in_vmem(kept), in_vmem(weights))


def flip_kernel(place_ref, own_ref, other_ref, after_ref, own_out, other_out, zero_ref):
    share = own_ref.shape[1] // 4
    for kept_ref, out_ref in ((own_ref, own_out), (other_ref, other_out)):
        for e in range(4):
            y = lax.rem(place_ref[2] + e, 4)
            edges = pl.ds(pl.multiple_of(y * share, share), share)
            for d in range(4):
                tile = kept_ref[pl.ds((4 - d) % 4 * PAIR, PAIR), edges]
                out_ref[e * share : (e + 1) * share, d * PAIR : (d + 1) * PAIR] = tile.T
    zero_ref[...] = jnp.zeros(zero_ref.shape, f32)


def flip(own, other, place, after):
    edges = own.shape[1]
    return call(
        flip_kernel,
        [
            pltpu.VMEM((edges, HALF), bf16),
            pltpu.VMEM((edges, HALF), bf16),
            jax.ShapeDtypeStruct((8, after.shape[1]), f32),
        ],
        [IN_SMEM, IN_VMEM, IN_VMEM, ANYWHERE],
        [IN_VMEM, IN_VMEM, IN_VMEM],
        16 * HALF * edges * 128,
    )(place, in_vmem(own), in_vmem(other), after)


def column_sums(low):
    return jnp.dot(jnp.ones((8, low.shape[0]), bf16), low, preferred_element_type=f32)


def add_loads(flipped_ref, low_ref, load, size):
    stride = low_ref.shape[0] // 4
    for d in range(4):
        low = low_ref[d * stride : d * stride + PAIR, :]
        load += jnp.dot(flipped_ref[:, d * PAIR : (d + 1) * PAIR], low, preferred_element_type=f32)
        size += column_sums(low)
    return load, size


def half_loads_kernel(flipped_ref, low_ref, load_ref, size_ref):
    load, size = add_loads(flipped_ref, low_ref, jnp.zeros(load_ref.shape, f32), jnp.zeros(size_ref.shape, f32))
    load_ref[...] = load
    size_ref[...] = size


def whole_loads_kernel(flipped_ref, low_ref, load_in, size_in, load_ref, power_ref):
    load, size = add_loads(flipped_ref, low_ref, load_in[...], size_in[...])
    power = jnp.floor(jnp.log2(jnp.maximum(size, 1e-30)))
    share = load.shape[0] // 4
    load_ref[:share, :] = load[:share]
    load_ref[share:, :] = load[share:] * jnp.exp2(11.0 - power[:1, :])
    power_ref[...] = power


def loads(kernel, flipped, low, *so_far):
    edges, scen = flipped.shape[0], low.shape[1]
    return call(
        kernel,
        [jax.ShapeDtypeStruct((edges, scen), f32), jax.ShapeDtypeStruct((8, scen), f32)],
        [IN_VMEM] * (2 + len(so_far)),
        [IN_VMEM, IN_VMEM],
        2 * HALF * edges * scen,
    )(in_vmem(flipped), low, *so_far)


def total_kernel(sums_own, sums_away, low_own, low_away, out_ref):
    totals = [jnp.zeros((32, BLOCK), f32) for _ in range(3)]
    stride = low_own.shape[0] // 4
    for sums_ref, low_ref in ((sums_own, low_own), (sums_away, low_away)):
        for d in range(4):
            sums = sums_ref[d * GATHERED + PAIR : (d + 1) * GATHERED, :]
            for j in range(3):
                low = low_ref[d * stride + j * BLOCK : d * stride + (j + 1) * BLOCK, :]
                totals[j] += jnp.dot(sums, low, preferred_element_type=f32)
    row = lax.broadcasted_iota(jnp.int32, (32, BLOCK), 0)
    total = jnp.zeros((32, BLOCK), f32)
    for j in range(3):
        total += jnp.where(row % 8 == j, totals[j], 0.0)
    out_ref[...] = jnp.full(out_ref.shape, jnp.sum(total), f32)


def total_load(sums_own, sums_away, low_own, low_away):
    return call(
        total_kernel,
        jax.ShapeDtypeStruct((8, low_own.shape[1]), f32),
        [IN_VMEM] * 4,
        IN_VMEM,
        10**8,
    )(sums_own, sums_away, low_own, low_away)


def bf16_parts(sums):
    parts = []
    left = sums
    for _ in range(3):
        part = lax.reduce_precision(left, 8, 7)
        left = left - part
        parts.append(part)
    return parts + [jnp.zeros_like(sums)]


def pack_sums(value):
    return jnp.concatenate([value[:PAIR]] + bf16_parts(value[PAIR:]), axis=0).astype(bf16)


def unpack_sums(value):
    value = value.astype(f32)
    sums = value[PAIR : PAIR + 8] + value[PAIR + 8 : PAIR + 16] + value[PAIR + 16 : PAIR + 24]
    return jnp.concatenate([value[:PAIR], sums], axis=0)


def pack_int16(value):
    top = jnp.max(value, axis=0, keepdims=True)
    power = jnp.ceil(jnp.log2(jnp.maximum(top, 1e-30)))
    code = jnp.round(value * jnp.exp2(16.0 - power)) - 32768.0
    code = jnp.clip(code, -32768.0, 32767.0)
    tile = jnp.broadcast_to(power, (16, value.shape[1]))
    return jnp.concatenate([code, tile], axis=0).astype(jnp.int32).astype(jnp.int16)


def unpack_int16(value):
    value = value.astype(jnp.int32).astype(f32)
    return (value[:-16] + 32768.0) * jnp.exp2(value[-16:-15] - 16.0)


def to_float16(value):
    return lax.reduce_precision(value, 5, 10)


def pack_part(load, power):
    return to_float16(jnp.concatenate([load, power, power], axis=0)).astype(jnp.float16)


def unpack_part(wire):
    wire = wire.astype(f32)
    return wire[:-16] * jnp.exp2(wire[-16:-15] - 11.0), wire[-16:-8]


def pack_load(load, power, total):
    load = load * jnp.exp2(11.0 - power[:1])
    scale = jnp.floor(jnp.log2(jnp.maximum(total, 1e-30)))
    total = total * jnp.exp2(-scale)
    high = to_float16(total)
    return to_float16(jnp.concatenate([load, power, scale, high, (total - high) * 1024.0], axis=0))


def update_kernel(place_ref, zero, one, two, three, current_ref, out_ref, low_ref, mean_ref):
    share = zero.shape[0] - 32
    powers, totals = [], []
    for wire in (zero, one, two, three):
        power, scale, high, low = (wire[share + 8 * n : share + 8 * n + 1, :] for n in range(4))
        powers.append(power)
        totals.append((high + low * (1.0 / 1024.0)) * jnp.exp2(scale))
    mean = ((totals[0] + totals[2]) + (totals[1] + totals[3])) * (1.0 / (EDGES * SCEN)) + 1e-06
    mean_ref[...] = jnp.broadcast_to(mean, mean_ref.shape)
    for d, wire in enumerate((zero, one, two, three)):
        y = lax.rem(place_ref[2] + d, 4)
        rows = pl.ds(pl.multiple_of(y * share, share), share)
        factor = -0.25 * jnp.exp2(powers[d] - 11.0) / mean
        new = current_ref[rows, :].astype(f32) * jnp.exp(wire[:share, :] * factor)
        out_ref[rows, :] = new
        low_ref[rows, :] = new.astype(bf16)


def update(wires, current, place, last):
    edges, scen = current.shape
    shape = jax.ShapeDtypeStruct if last else pltpu.VMEM
    return call(
        update_kernel,
        [shape((edges, scen), f32), pltpu.VMEM((edges, scen), bf16), jax.ShapeDtypeStruct((8, scen), f32)],
        [IN_SMEM] + [IN_VMEM] * 5,
        [IN_VMEM] * 3,
        10**7,
    )(place, *wires, current)


def ring(n, d, stride=1):
    return [(i, (i + d * stride) % n) for i in range(n)]


def swap(bit):
    return [(i, i ^ bit) for i in range(16)]


def pair_sum(value, axis, bit):
    return value + lax.ppermute(value, axis, [(i, i ^ bit) for i in range(4)])


def sum_four(parts):
    zero, one, two, three = parts
    return (zero + two) + (one + three)


def body(coverage, block_mask, edge_prior, test_cost):
    at = lax.axis_index("col")
    x, z, core = at // 4, (at // 2) % 2, at % 2
    place = jnp.stack([x, core, lax.axis_index("row")]).astype(jnp.int32)
    costs = test_cost.reshape(4, 2, 2, CHUNK, test_cost.shape[1])
    cost = lax.dynamic_slice(costs, (x, 0, core, 0, 0), (1, 2, 1, CHUNK, costs.shape[-1]))
    cost = cost.reshape(PAIR, costs.shape[-1]).astype(f32)

    current = edge_prior
    for iteration in range(ITERS):
        first = iteration == 0
        pack, unpack = (pack_sums, unpack_sums) if first else (pack_int16, unpack_int16)
        with jax.named_scope("scores"):
            if first:
                away, kept_away, here, kept_here = first_scores(coverage, block_mask, edge_prior, place)
            else:
                away = later_scores(kept_away, low_weights)
                here = later_scores(kept_here, low_weights)
            here = here + lax.ppermute(away, "col", swap(1))
            here = here.reshape(4, -1, here.shape[-1])
        with jax.named_scope("sum_x"):
            parts = [unpack(lax.ppermute(pack(here[d]), "col", ring(16, d, 4))) for d in (1, 2, 3)]
            scores = sum_four([here[0]] + parts)
        if first:
            with jax.named_scope("flip"):
                flipped_here, flipped_away, zero = flip(kept_here, kept_away, place, scores)
                cost = cost + zero[:1]
        with jax.named_scope("sum_z"):
            scores = scores + unpack(lax.ppermute(pack(scores), "col", swap(2)))
            ratios = scores[:PAIR] / cost
            low_ratios = ratios.astype(bf16)
            if first:
                sums = [part.astype(bf16) for part in bf16_parts(scores[PAIR:])]
                low_ratios = jnp.concatenate([low_ratios] + sums, axis=0)
        with jax.named_scope("gather"):
            lows = [low_ratios] + [lax.ppermute(low_ratios, "col", ring(16, d, 4)) for d in (1, 2, 3)]
            low_here = jnp.concatenate(lows, axis=0)
            low_away = lax.ppermute(low_here, "col", swap(1))
            if first:
                sums_here, sums_away = low_here, low_away
        with jax.named_scope("total"):
            total = total_load(sums_here, sums_away, low_here, low_away)
            total = pair_sum(pair_sum(total, "depth", 1), "depth", 2)
        with jax.named_scope("loads"):
            half, size = loads(half_loads_kernel, flipped_here, low_here)
            load, power = loads(whole_loads_kernel, flipped_away, low_away, half, size)
        with jax.named_scope("sum_y"):
            share = load.shape[0] // 4
            parts, powers = [load[:share]], [power]
            for d in (1, 2, 3):
                wire = pack_part(load[d * share : (d + 1) * share], power)
                part, exponent = unpack_part(lax.ppermute(wire, "row", ring(4, d)))
                parts.append(part)
                powers.append(exponent)
            power = jnp.maximum(jnp.maximum(powers[0], powers[1]), jnp.maximum(powers[2], powers[3])) + 2.0
        with jax.named_scope("gather_y"):
            wire = pack_load(sum_four(parts), power, total)
            sent = wire.astype(jnp.float16)
            wires = [wire] + [lax.ppermute(sent, "row", ring(4, -d)).astype(f32) for d in (1, 2, 3)]
        with jax.named_scope("update"):
            current, low_weights, load_mean = update(wires, current, place, iteration == ITERS - 1)
    own = lax.dynamic_slice_in_dim(ratios, z * CHUNK, CHUNK, 0)
    primal = TESTS * own / load_mean[:1]
    return (current, primal)


def solution(mesh):
    placed = (P("row", "col"), P("row", "col"), P("col", "depth"), P("row", "depth"))
    return jax.shard_map(
        body,
        mesh=mesh,
        in_specs=placed,
        out_specs=(P("col", "depth"), P(("row", "col"), "depth")),
        check_vma=False,
    )
```

```python
import functools

import jax
import jax.numpy as jnp
from jax import lax
from jax.experimental import pallas as pl
from jax.experimental.pallas import tpu as pltpu
from jax.sharding import PartitionSpec as P

EDGES = 16384
SCEN = 512
BLOCK = 128
ITERS = 2
TESTS = 12288
CHUNK = 192
PAIR = 2 * CHUNK
HALF = 4 * PAIR
WITH_SUMS = PAIR + 8
GATHERED = PAIR + 32
VMEM_LIMIT = 16 * 1024 * 1024
IN_VMEM = pl.BlockSpec(memory_space=pltpu.VMEM)
IN_SMEM = pl.BlockSpec(memory_space=pltpu.SMEM)
ANYWHERE = pl.BlockSpec(memory_space=pl.ANY)
IN_HBM = pl.BlockSpec(memory_space=pltpu.HBM)
f32 = jnp.float32
bf16 = jnp.bfloat16


def call(kernel, out_shape, in_specs, out_specs, flops, scratch=()):
    return pl.pallas_call(
        kernel,
        in_specs=in_specs,
        out_specs=out_specs,
        out_shape=out_shape,
        scratch_shapes=list(scratch),
        compiler_params=pltpu.CompilerParams(vmem_limit_bytes=VMEM_LIMIT),
        cost_estimate=pl.CostEstimate(flops=flops, bytes_accessed=flops // 400, transcendentals=0),
    )


def in_vmem(value):
    return pltpu.with_memory_space_constraint(value, pltpu.VMEM)


def in_hbm(value):
    return pltpu.with_memory_space_constraint(value, pltpu.HBM)


def tests_of(kept_ref, d, core, edges=slice(None)):
    at = [pl.multiple_of((d * 4 + z * 2 + core) * CHUNK, CHUNK) for z in range(2)]
    return jnp.concatenate([kept_ref[pl.ds(a, CHUNK), edges] for a in at], axis=0)


def scores_and_sums(kept, weights, out_ref, d):
    at = d * WITH_SUMS
    out_ref[at : at + PAIR, :] = jnp.dot(kept, weights, preferred_element_type=f32)
    ones = jnp.ones((8, kept.shape[1]), bf16)
    sums = lax.dot_general(ones, kept, (((1,), (1,)), ((), ())), preferred_element_type=f32)
    out_ref[at + PAIR : at + WITH_SUMS, :] = jnp.concatenate(
        [sums[:1, j * BLOCK : (j + 1) * BLOCK] for j in range(3)] + [jnp.zeros((5, BLOCK), f32)], axis=0
    )


def first_scores_kernel(place_ref, mask_ref, cover_ref, prior_ref, out_ref, kept_ref, weights_ref, rows_ref, tiles_ref, sems):
    tiles = pltpu.make_async_copy(mask_ref, tiles_ref, sems.at[4])
    tiles.start()
    copies = []
    for d in range(4):
        rows = pl.ds(pl.multiple_of(lax.rem(place_ref[0] + d, 4) * 4 * CHUNK, CHUNK), 4 * CHUNK)
        copy = pltpu.make_async_copy(
            cover_ref.at[rows, :], kept_ref.at[pl.ds(d * 4 * CHUNK, 4 * CHUNK), :], sems.at[d]
        )
        copy.start()
        copies.append(copy)
        if d == 0:
            weights = pltpu.make_async_copy(prior_ref, weights_ref, sems.at[5])
            weights.start()
    edges = cover_ref.shape[1]
    tiles.wait()
    column = lax.broadcasted_iota(jnp.int32, (tiles_ref.shape[0], edges), 1) // BLOCK
    spread = column == lax.broadcasted_iota(jnp.int32, column.shape, 0)
    rows_ref[...] = lax.dot_general(
        tiles_ref[...].astype(f32), spread.astype(f32), (((0,), (0,)), ((), ())), preferred_element_type=f32
    )
    weights.wait()
    blocks = 4 * CHUNK // BLOCK
    for d in range(4):
        copies[d].wait()
        first = lax.rem(place_ref[0] + d, 4) * blocks
        for b in range(blocks):
            entry = jnp.broadcast_to(rows_ref[pl.ds(first + b, 1), :], (16, edges)).astype(bf16)
            for k in range(BLOCK // 16):
                at = (d * blocks + b) * BLOCK + k * 16
                kept_ref[at : at + 16, :] = kept_ref[at : at + 16, :] * entry
        scores_and_sums(tests_of(kept_ref, d, 1 - place_ref[1]), weights_ref[...], out_ref, d)


def own_scores_kernel(place_ref, kept_ref, weights_ref, out_ref):
    for d in range(4):
        scores_and_sums(tests_of(kept_ref, d, place_ref[1]), weights_ref[...], out_ref, d)


def first_scores(cover, mask, prior, place):
    edges, scen = prior.shape
    away, kept, weights = call(
        first_scores_kernel,
        [
            pltpu.VMEM((4 * WITH_SUMS, scen), f32),
            pltpu.VMEM(cover.shape, bf16),
            pltpu.VMEM(prior.shape, bf16),
        ],
        [IN_SMEM, IN_HBM, IN_HBM, IN_HBM],
        [IN_VMEM] * 3,
        2 * HALF * edges * scen,
        [
            pltpu.VMEM((mask.shape[0], edges), f32),
            pltpu.VMEM(mask.shape[::-1], mask.dtype),
            pltpu.SemaphoreType.DMA((6,)),
        ],
    )(place, in_hbm(mask.T), in_hbm(cover), in_hbm(prior))
    here = call(
        own_scores_kernel,
        pltpu.VMEM((4 * WITH_SUMS, scen), f32),
        [IN_SMEM, IN_VMEM, IN_VMEM],
        IN_VMEM,
        2 * HALF * edges * scen,
    )(place, in_vmem(kept), in_vmem(weights))
    return away, here, kept, weights


def scores_kernel(own, place_ref, kept_ref, weights_ref, out_ref):
    core = place_ref[1] if own else 1 - place_ref[1]
    for d in range(4):
        out_ref[d * PAIR : (d + 1) * PAIR, :] = jnp.dot(
            tests_of(kept_ref, d, core), weights_ref[...], preferred_element_type=f32
        )


def later_scores(own, kept, weights, place):
    edges, scen = weights.shape
    return call(
        functools.partial(scores_kernel, own),
        pltpu.VMEM((HALF, scen), f32),
        [IN_SMEM, IN_VMEM, IN_VMEM],
        IN_VMEM,
        2 * HALF * edges * scen,
    )(place, in_vmem(kept), in_vmem(weights))


def flip_kernel(place_ref, kept_ref, cost_ref, after_ref, own_out, other_out, cost_out, cost_in, sems):
    copies = []
    for z in range(2):
        at = pl.multiple_of((place_ref[0] * 4 + z * 2 + place_ref[1]) * CHUNK, CHUNK)
        copy = pltpu.make_async_copy(
            cost_ref.at[pl.ds(at, CHUNK), :], cost_in.at[pl.ds(z * CHUNK, CHUNK), :], sems.at[z]
        )
        copy.start()
        copies.append(copy)
    share = kept_ref.shape[1] // 4
    for half, out_ref in enumerate((own_out, other_out)):
        core = 1 - place_ref[1] if half else place_ref[1]
        for e in range(4):
            y = lax.rem(place_ref[2] + e, 4)
            edges = pl.ds(pl.multiple_of(y * share, share), share)
            for d in range(4):
                tile = tests_of(kept_ref, (4 - d) % 4, core, edges)
                out_ref[e * share : (e + 1) * share, d * PAIR : (d + 1) * PAIR] = tile.T
    for copy in copies:
        copy.wait()
    cost_out[...] = cost_in[...].astype(f32)


def flip(kept, cost, place, after):
    edges = kept.shape[1]
    return call(
        flip_kernel,
        [
            pltpu.VMEM((edges, HALF), bf16),
            pltpu.VMEM((edges, HALF), bf16),
            pltpu.VMEM((PAIR, cost.shape[1]), f32),
        ],
        [IN_SMEM, IN_VMEM, IN_HBM, ANYWHERE],
        [IN_VMEM, IN_VMEM, IN_VMEM],
        16 * HALF * edges * 128,
        [pltpu.VMEM((PAIR, cost.shape[1]), cost.dtype), pltpu.SemaphoreType.DMA((2,))],
    )(place, in_vmem(kept), in_hbm(cost), after)


def column_sums(low):
    return jnp.dot(jnp.ones((8, low.shape[0]), bf16), low, preferred_element_type=f32)


def add_loads(flipped_ref, low_ref, load, size):
    stride = low_ref.shape[0] // 4
    for d in range(4):
        low = low_ref[d * stride : d * stride + PAIR, :]
        load += jnp.dot(flipped_ref[:, d * PAIR : (d + 1) * PAIR], low, preferred_element_type=f32)
        size += column_sums(low)
    return load, size


def half_loads_kernel(flipped_ref, low_ref, load_ref, size_ref):
    load, size = add_loads(flipped_ref, low_ref, jnp.zeros(load_ref.shape, f32), jnp.zeros(size_ref.shape, f32))
    load_ref[...] = load
    size_ref[...] = size


def whole_loads_kernel(flipped_ref, low_ref, load_in, size_in, load_ref, power_ref):
    load, size = add_loads(flipped_ref, low_ref, load_in[...], size_in[...])
    power = jnp.floor(jnp.log2(jnp.maximum(size, 1e-30)))
    share = load.shape[0] // 4
    load_ref[:share, :] = load[:share]
    load_ref[share:, :] = load[share:] * jnp.exp2(11.0 - power[:1, :])
    power_ref[...] = power


def loads(kernel, flipped, low, *so_far):
    edges, scen = flipped.shape[0], low.shape[1]
    return call(
        kernel,
        [jax.ShapeDtypeStruct((edges, scen), f32), jax.ShapeDtypeStruct((8, scen), f32)],
        [IN_VMEM] * (2 + len(so_far)),
        [IN_VMEM, IN_VMEM],
        2 * HALF * edges * scen,
    )(in_vmem(flipped), low, *so_far)


def total_kernel(sums_own, sums_away, low_own, low_away, out_ref):
    totals = [jnp.zeros((32, BLOCK), f32) for _ in range(3)]
    stride = low_own.shape[0] // 4
    for sums_ref, low_ref in ((sums_own, low_own), (sums_away, low_away)):
        for d in range(4):
            sums = sums_ref[d * GATHERED + PAIR : (d + 1) * GATHERED, :]
            for j in range(3):
                low = low_ref[d * stride + j * BLOCK : d * stride + (j + 1) * BLOCK, :]
                totals[j] += jnp.dot(sums, low, preferred_element_type=f32)
    row = lax.broadcasted_iota(jnp.int32, (32, BLOCK), 0)
    total = jnp.zeros((32, BLOCK), f32)
    for j in range(3):
        total += jnp.where(row % 8 == j, totals[j], 0.0)
    out_ref[...] = jnp.full(out_ref.shape, jnp.sum(total), f32)


def total_load(sums_own, sums_away, low_own, low_away):
    return call(
        total_kernel,
        jax.ShapeDtypeStruct((8, low_own.shape[1]), f32),
        [IN_VMEM] * 4,
        IN_VMEM,
        10**8,
    )(sums_own, sums_away, low_own, low_away)


def bf16_parts(sums):
    parts = []
    left = sums
    for _ in range(3):
        part = lax.reduce_precision(left, 8, 7)
        left = left - part
        parts.append(part)
    return parts + [jnp.zeros_like(sums)]


def pack_sums(value):
    return jnp.concatenate([value[:PAIR]] + bf16_parts(value[PAIR:]), axis=0).astype(bf16)


def unpack_sums(value):
    value = value.astype(f32)
    sums = value[PAIR : PAIR + 8] + value[PAIR + 8 : PAIR + 16] + value[PAIR + 16 : PAIR + 24]
    return jnp.concatenate([value[:PAIR], sums], axis=0)


def pack_int16(value):
    top = jnp.max(value, axis=0, keepdims=True)
    power = jnp.ceil(jnp.log2(jnp.maximum(top, 1e-30)))
    code = jnp.round(value * jnp.exp2(16.0 - power)) - 32768.0
    code = jnp.clip(code, -32768.0, 32767.0)
    tile = jnp.broadcast_to(power, (16, value.shape[1]))
    return jnp.concatenate([code, tile], axis=0).astype(jnp.int32).astype(jnp.int16)


def unpack_int16(value):
    value = value.astype(jnp.int32).astype(f32)
    return (value[:-16] + 32768.0) * jnp.exp2(value[-16:-15] - 16.0)


def to_float16(value):
    return lax.reduce_precision(value, 5, 10)


def pack_part(load, power, total):
    return jnp.concatenate([load, power] + total, axis=0).astype(jnp.float16)


def float16_parts(total):
    scale = jnp.floor(jnp.log2(jnp.maximum(total, 1e-30)))
    total = total * jnp.exp2(-scale)
    high = to_float16(total)
    return [scale, high, to_float16((total - high) * 1024.0)]


def from_parts(scale, high, low):
    return (high + low * (1.0 / 1024.0)) * jnp.exp2(scale)


def unpack_part(wire):
    wire = wire.astype(f32)
    share = wire.shape[0] - 32
    power, *total = (wire[at : at + 8] for at in range(share, share + 32, 8))
    return wire[:share] * jnp.exp2(power[:1] - 11.0), power, from_parts(*total)


def pack_load(load, power):
    return to_float16(jnp.concatenate([load * jnp.exp2(11.0 - power[:1]), power, power], axis=0))


def update_kernel(last, place_ref, zero, one, two, three, total_ref, current_ref, *rest):
    share = zero.shape[0] - 16
    mean = total_ref[:1, :] * (1.0 / (EDGES * SCEN)) + 1e-06
    if last:
        ratios_ref, out_ref, primal_ref = rest
        own = ratios_ref[pl.ds(pl.multiple_of(place_ref[3] * CHUNK, CHUNK), CHUNK), :]
        primal_ref[...] = TESTS * own / mean
    else:
        out_ref, low_ref = rest
    for d, wire in enumerate((zero, one, two, three)):
        y = lax.rem(place_ref[2] + d, 4)
        rows = pl.ds(pl.multiple_of(y * share, share), share)
        factor = -0.25 * jnp.exp2(wire[share : share + 1, :] - 11.0) / mean
        new = current_ref[rows, :].astype(f32) * jnp.exp(wire[:share, :] * factor)
        out_ref[rows, :] = new
        if not last:
            low_ref[rows, :] = new.astype(bf16)


def update(wires, total, current, place, ratios=None):
    edges, scen = current.shape
    last = ratios is not None
    if last:
        shapes = [jax.ShapeDtypeStruct((edges, scen), f32), jax.ShapeDtypeStruct((CHUNK, scen), f32)]
    else:
        shapes = [pltpu.VMEM((edges, scen), f32), pltpu.VMEM((edges, scen), bf16)]
    return call(
        functools.partial(update_kernel, last),
        shapes,
        [IN_SMEM] + [IN_VMEM] * (7 if last else 6),
        [IN_VMEM] * 2,
        10**7,
    )(place, *wires, total, in_vmem(current), *([ratios] if last else []))


def ring(n, d, stride=1):
    return [(i, (i + d * stride) % n) for i in range(n)]


def swap(bit):
    return [(i, i ^ bit) for i in range(16)]


def pair_sum(value, axis, bit):
    return value + lax.ppermute(value, axis, [(i, i ^ bit) for i in range(4)])


def sum_four(parts):
    zero, one, two, three = parts
    return (zero + two) + (one + three)


def body(coverage, block_mask, edge_prior, test_cost):
    at = lax.axis_index("col")
    x, z, core = at // 4, (at // 2) % 2, at % 2
    place = jnp.stack([x, core, lax.axis_index("row"), z]).astype(jnp.int32)
    for iteration in range(ITERS):
        first = iteration == 0
        pack, unpack = (pack_sums, unpack_sums) if first else (pack_int16, unpack_int16)
        with jax.named_scope("scores"):
            if first:
                away, here, kept, low_weights = first_scores(coverage, block_mask, edge_prior, place)
                current = low_weights
            else:
                away = later_scores(False, kept, low_weights, place)
                here = later_scores(True, kept, low_weights, place)
            here = here + lax.ppermute(away, "col", swap(1))
            here = here.reshape(4, -1, here.shape[-1])
        with jax.named_scope("sum_x"):
            parts = [unpack(lax.ppermute(pack(here[d]), "col", ring(16, d, 4))) for d in (1, 2, 3)]
            scores = sum_four([here[0]] + parts)
        if first:
            with jax.named_scope("flip"):
                flipped_here, flipped_away, cost = flip(kept, test_cost, place, scores)
        with jax.named_scope("sum_z"):
            scores = scores + unpack(lax.ppermute(pack(scores), "col", swap(2)))
            ratios = scores[:PAIR] / cost
            low_ratios = ratios.astype(bf16)
            if first:
                sums = [part.astype(bf16) for part in bf16_parts(scores[PAIR:])]
                low_ratios = jnp.concatenate([low_ratios] + sums, axis=0)
        with jax.named_scope("gather"):
            lows = [low_ratios] + [lax.ppermute(low_ratios, "col", ring(16, d, 4)) for d in (1, 2, 3)]
            low_here = jnp.concatenate(lows, axis=0)
            low_away = lax.ppermute(low_here, "col", swap(1))
            if first:
                sums_here, sums_away = low_here, low_away
        with jax.named_scope("total"):
            total = total_load(sums_here, sums_away, low_here, low_away)
            total = float16_parts(pair_sum(total, "depth", 1))
        with jax.named_scope("loads"):
            half, size = loads(half_loads_kernel, flipped_here, low_here)
            load, power = loads(whole_loads_kernel, flipped_away, low_away, half, size)
        with jax.named_scope("sum_y"):
            share = load.shape[0] // 4
            parts = [(load[:share], power, from_parts(*total))]
            for d in (1, 2, 3):
                wire = pack_part(load[d * share : (d + 1) * share], power, total)
                parts.append(unpack_part(lax.ppermute(wire, "row", ring(4, d))))
            part, powers, totals = zip(*parts, strict=True)
            power = jnp.maximum(jnp.maximum(powers[0], powers[1]), jnp.maximum(powers[2], powers[3])) + 2.0
        with jax.named_scope("gather_y"):
            wire = pack_load(sum_four(part), power)
            sent = wire.astype(jnp.float16)
            wires = [wire] + [lax.ppermute(sent, "row", ring(4, -d)).astype(f32) for d in (1, 2, 3)]
        with jax.named_scope("total"):
            total = pair_sum(sum_four(totals), "depth", 2)
        with jax.named_scope("update"):
            if iteration < ITERS - 1:
                current, low_weights = update(wires, total, current, place)
            else:
                current, primal = update(wires, total, current, place, ratios)
    return (current, primal)


def solution(mesh):
    placed = (P("row", "col"), P("row", "col"), P("col", "depth"), P("row", "depth"))
    return jax.shard_map(
        body,
        mesh=mesh,
        in_specs=placed,
        out_specs=(P("col", "depth"), P(("row", "col"), "depth")),
        check_vma=False,
    )
```

```python
import functools

import jax
import jax.numpy as jnp
from jax import lax
from jax.experimental import pallas as pl
from jax.experimental.pallas import tpu as pltpu
from jax.sharding import PartitionSpec as P

EDGES = 16384
SCEN = 512
BLOCK = 128
ITERS = 2
TESTS = 12288
CHUNK = 192
PAIR = 2 * CHUNK
HALF = 4 * PAIR
WITH_SUMS = PAIR + 8
GATHERED = PAIR + 32
VMEM_LIMIT = 16 * 1024 * 1024
IN_VMEM = pl.BlockSpec(memory_space=pltpu.VMEM)
IN_SMEM = pl.BlockSpec(memory_space=pltpu.SMEM)
ANYWHERE = pl.BlockSpec(memory_space=pl.ANY)
IN_HBM = pl.BlockSpec(memory_space=pltpu.HBM)
f32 = jnp.float32
bf16 = jnp.bfloat16


def call(kernel, out_shape, in_specs, out_specs, flops, scratch=()):
    return pl.pallas_call(
        kernel,
        in_specs=in_specs,
        out_specs=out_specs,
        out_shape=out_shape,
        scratch_shapes=list(scratch),
        compiler_params=pltpu.CompilerParams(vmem_limit_bytes=VMEM_LIMIT),
        cost_estimate=pl.CostEstimate(flops=flops, bytes_accessed=flops // 400, transcendentals=0),
    )


def in_vmem(value):
    return pltpu.with_memory_space_constraint(value, pltpu.VMEM)


def in_hbm(value):
    return pltpu.with_memory_space_constraint(value, pltpu.HBM)


def tests_of(kept_ref, d, half, edges=slice(None)):
    tests = kept_ref[half * 4 + d, :, :, edges]
    return tests.reshape(PAIR, tests.shape[-1])


def scores_and_sums(kept, weights, out_ref, d):
    at = d * WITH_SUMS
    out_ref[at : at + PAIR, :] = jnp.dot(kept, weights, preferred_element_type=f32)
    ones = jnp.ones((8, kept.shape[1]), bf16)
    sums = lax.dot_general(ones, kept, (((1,), (1,)), ((), ())), preferred_element_type=f32)
    out_ref[at + PAIR : at + WITH_SUMS, :] = jnp.concatenate(
        [sums[:1, j * BLOCK : (j + 1) * BLOCK] for j in range(3)] + [jnp.zeros((5, BLOCK), f32)], axis=0
    )


def first_scores_kernel(place_ref, mask_ref, cover_ref, prior_ref, out_ref, kept_ref, weights_ref, rows_ref, tiles_ref, sems):
    tiles = pltpu.make_async_copy(mask_ref, tiles_ref, sems.at[8])
    tiles.start()
    copies = {}
    for half in (1, 0):
        core = 1 - place_ref[1] if half else place_ref[1]
        for d in range(4):
            x = lax.rem(place_ref[0] + d, 4)
            copy = pltpu.make_async_copy(
                cover_ref.at[pl.ds(2 * x, 2), core], kept_ref.at[half * 4 + d], sems.at[half * 4 + d]
            )
            copy.start()
            copies[half, d] = copy
        if half:
            weights = pltpu.make_async_copy(prior_ref, weights_ref, sems.at[9])
            weights.start()
    edges = cover_ref.shape[-1]
    tiles.wait()
    column = lax.broadcasted_iota(jnp.int32, (tiles_ref.shape[0], edges), 1) // BLOCK
    spread = column == lax.broadcasted_iota(jnp.int32, column.shape, 0)
    rows_ref[...] = lax.dot_general(
        tiles_ref[...].astype(f32), spread.astype(f32), (((0,), (0,)), ((), ())), preferred_element_type=f32
    )
    weights.wait()
    lines = BLOCK // 2
    for half in (1, 0):
        core = 1 - place_ref[1] if half else place_ref[1]
        for d in range(4):
            copies[half, d].wait()
            for z in range(2):
                chunk = lax.rem(place_ref[0] + d, 4) * 4 + z * 2 + core
                for j in range(CHUNK // lines):
                    block_row = (chunk * (CHUNK // lines) + j) // 2
                    entry = jnp.broadcast_to(rows_ref[pl.ds(block_row, 1), :], (16, edges)).astype(bf16)
                    for k in range(lines // 16):
                        at = slice(j * lines + k * 16, j * lines + k * 16 + 16)
                        kept_ref[half * 4 + d, z, at, :] = kept_ref[half * 4 + d, z, at, :] * entry
            if half:
                scores_and_sums(tests_of(kept_ref, d, half), weights_ref[...], out_ref, d)


def own_scores_kernel(kept_ref, weights_ref, out_ref):
    for d in range(4):
        scores_and_sums(tests_of(kept_ref, d, 0), weights_ref[...], out_ref, d)


def first_scores(cover, mask, prior, place):
    edges, scen = prior.shape
    away, kept, weights = call(
        first_scores_kernel,
        [
            pltpu.VMEM((4 * WITH_SUMS, scen), f32),
            pltpu.VMEM((8, 2, CHUNK, edges), bf16),
            pltpu.VMEM(prior.shape, bf16),
        ],
        [IN_SMEM, IN_HBM, IN_HBM, IN_HBM],
        [IN_VMEM] * 3,
        2 * HALF * edges * scen,
        [
            pltpu.VMEM((mask.shape[0], edges), f32),
            pltpu.VMEM(mask.shape[::-1], mask.dtype),
            pltpu.SemaphoreType.DMA((10,)),
        ],
    )(place, in_hbm(mask.T), in_hbm(cover.reshape(-1, 2, CHUNK, edges)), in_hbm(prior))
    here = call(
        own_scores_kernel,
        pltpu.VMEM((4 * WITH_SUMS, scen), f32),
        [IN_VMEM, IN_VMEM],
        IN_VMEM,
        2 * HALF * edges * scen,
    )(in_vmem(kept), in_vmem(weights))
    return away, here, kept, weights


def scores_kernel(half, kept_ref, weights_ref, out_ref):
    for d in range(4):
        out_ref[d * PAIR : (d + 1) * PAIR, :] = jnp.dot(
            tests_of(kept_ref, d, half), weights_ref[...], preferred_element_type=f32
        )


def later_scores(half, kept, weights):
    edges, scen = weights.shape
    return call(
        functools.partial(scores_kernel, half),
        pltpu.VMEM((HALF, scen), f32),
        [IN_VMEM, IN_VMEM],
        IN_VMEM,
        2 * HALF * edges * scen,
    )(in_vmem(kept), in_vmem(weights))


def flip_kernel(place_ref, kept_ref, cost_ref, after_ref, own_out, other_out, cost_out, cost_in, sems):
    copies = []
    for z in range(2):
        at = pl.multiple_of((place_ref[0] * 4 + z * 2 + place_ref[1]) * CHUNK, CHUNK)
        copy = pltpu.make_async_copy(
            cost_ref.at[pl.ds(at, CHUNK), :], cost_in.at[pl.ds(z * CHUNK, CHUNK), :], sems.at[z]
        )
        copy.start()
        copies.append(copy)
    share = kept_ref.shape[-1] // 4
    for half, out_ref in enumerate((own_out, other_out)):
        for e in range(4):
            y = lax.rem(place_ref[2] + e, 4)
            edges = pl.ds(pl.multiple_of(y * share, share), share)
            for d in range(4):
                tile = tests_of(kept_ref, (4 - d) % 4, half, edges)
                out_ref[e * share : (e + 1) * share, d * PAIR : (d + 1) * PAIR] = tile.T
    for copy in copies:
        copy.wait()
    cost_out[...] = cost_in[...].astype(f32)


def flip(kept, cost, place, after):
    edges = kept.shape[-1]
    return call(
        flip_kernel,
        [
            pltpu.VMEM((edges, HALF), bf16),
            pltpu.VMEM((edges, HALF), bf16),
            pltpu.VMEM((PAIR, cost.shape[1]), f32),
        ],
        [IN_SMEM, IN_VMEM, IN_HBM, ANYWHERE],
        [IN_VMEM, IN_VMEM, IN_VMEM],
        16 * HALF * edges * 128,
        [pltpu.VMEM((PAIR, cost.shape[1]), cost.dtype), pltpu.SemaphoreType.DMA((2,))],
    )(place, in_vmem(kept), in_hbm(cost), after)


def column_sums(low):
    return jnp.dot(jnp.ones((8, low.shape[0]), bf16), low, preferred_element_type=f32)


def add_loads(flipped_ref, low_ref, load, size):
    stride = low_ref.shape[0] // 4
    for d in range(4):
        low = low_ref[d * stride : d * stride + PAIR, :]
        load += jnp.dot(flipped_ref[:, d * PAIR : (d + 1) * PAIR], low, preferred_element_type=f32)
        size += column_sums(low)
    return load, size


def half_loads_kernel(flipped_ref, low_ref, load_ref, size_ref):
    load, size = add_loads(flipped_ref, low_ref, jnp.zeros(load_ref.shape, f32), jnp.zeros(size_ref.shape, f32))
    load_ref[...] = load
    size_ref[...] = size


def whole_loads_kernel(flipped_ref, low_ref, load_in, size_in, load_ref, power_ref):
    load, size = add_loads(flipped_ref, low_ref, load_in[...], size_in[...])
    power = jnp.floor(jnp.log2(jnp.maximum(size, 1e-30)))
    share = load.shape[0] // 4
    load_ref[:share, :] = load[:share]
    load_ref[share:, :] = load[share:] * jnp.exp2(11.0 - power[:1, :])
    power_ref[...] = power


def loads(kernel, flipped, low, *so_far):
    edges, scen = flipped.shape[0], low.shape[1]
    return call(
        kernel,
        [jax.ShapeDtypeStruct((edges, scen), f32), jax.ShapeDtypeStruct((8, scen), f32)],
        [IN_VMEM] * (2 + len(so_far)),
        [IN_VMEM, IN_VMEM],
        2 * HALF * edges * scen,
    )(in_vmem(flipped), low, *so_far)


def total_kernel(sums_own, sums_away, low_own, low_away, out_ref):
    totals = [jnp.zeros((32, BLOCK), f32) for _ in range(3)]
    stride = low_own.shape[0] // 4
    for sums_ref, low_ref in ((sums_own, low_own), (sums_away, low_away)):
        for d in range(4):
            sums = sums_ref[d * GATHERED + PAIR : (d + 1) * GATHERED, :]
            for j in range(3):
                low = low_ref[d * stride + j * BLOCK : d * stride + (j + 1) * BLOCK, :]
                totals[j] += jnp.dot(sums, low, preferred_element_type=f32)
    row = lax.broadcasted_iota(jnp.int32, (32, BLOCK), 0)
    total = jnp.zeros((32, BLOCK), f32)
    for j in range(3):
        total += jnp.where(row % 8 == j, totals[j], 0.0)
    out_ref[...] = jnp.full(out_ref.shape, jnp.sum(total), f32)


def total_load(sums_own, sums_away, low_own, low_away):
    return call(
        total_kernel,
        jax.ShapeDtypeStruct((8, low_own.shape[1]), f32),
        [IN_VMEM] * 4,
        IN_VMEM,
        10**8,
    )(sums_own, sums_away, low_own, low_away)


def bf16_parts(sums):
    parts = []
    left = sums
    for _ in range(3):
        part = lax.reduce_precision(left, 8, 7)
        left = left - part
        parts.append(part)
    return parts + [jnp.zeros_like(sums)]


def pack_sums(value):
    return jnp.concatenate([value[:PAIR]] + bf16_parts(value[PAIR:]), axis=0).astype(bf16)


def unpack_sums(value):
    value = value.astype(f32)
    sums = value[PAIR : PAIR + 8] + value[PAIR + 8 : PAIR + 16] + value[PAIR + 16 : PAIR + 24]
    return jnp.concatenate([value[:PAIR], sums], axis=0)


def pack_int16(value):
    top = jnp.max(value, axis=0, keepdims=True)
    power = jnp.ceil(jnp.log2(jnp.maximum(top, 1e-30)))
    code = jnp.round(value * jnp.exp2(16.0 - power)) - 32768.0
    code = jnp.clip(code, -32768.0, 32767.0)
    tile = jnp.broadcast_to(power, (16, value.shape[1]))
    return jnp.concatenate([code, tile], axis=0).astype(jnp.int32).astype(jnp.int16)


def unpack_int16(value):
    value = value.astype(jnp.int32).astype(f32)
    return (value[:-16] + 32768.0) * jnp.exp2(value[-16:-15] - 16.0)


def to_float16(value):
    return lax.reduce_precision(value, 5, 10)


def pack_part(load, power, total):
    return jnp.concatenate([load, power] + total, axis=0).astype(jnp.float16)


def float16_parts(total):
    scale = jnp.floor(jnp.log2(jnp.maximum(total, 1e-30)))
    total = total * jnp.exp2(-scale)
    high = to_float16(total)
    return [scale, high, to_float16((total - high) * 1024.0)]


def from_parts(scale, high, low):
    return (high + low * (1.0 / 1024.0)) * jnp.exp2(scale)


def unpack_part(wire):
    wire = wire.astype(f32)
    share = wire.shape[0] - 32
    power, *total = (wire[at : at + 8] for at in range(share, share + 32, 8))
    return wire[:share] * jnp.exp2(power[:1] - 11.0), power, from_parts(*total)


def pack_load(load, power):
    return to_float16(jnp.concatenate([load * jnp.exp2(11.0 - power[:1]), power, power], axis=0))


def update_kernel(last, place_ref, zero, one, two, three, total_ref, current_ref, *rest):
    share = zero.shape[0] - 16
    mean = total_ref[:1, :] * (1.0 / (EDGES * SCEN)) + 1e-06
    if last:
        ratios_ref, out_ref, primal_ref = rest
        own = ratios_ref[pl.ds(pl.multiple_of(place_ref[3] * CHUNK, CHUNK), CHUNK), :]
        primal_ref[...] = TESTS * own / mean
    else:
        out_ref, low_ref = rest
    for d, wire in enumerate((zero, one, two, three)):
        y = lax.rem(place_ref[2] + d, 4)
        rows = pl.ds(pl.multiple_of(y * share, share), share)
        factor = -0.25 * jnp.exp2(wire[share : share + 1, :] - 11.0) / mean
        new = current_ref[rows, :].astype(f32) * jnp.exp(wire[:share, :] * factor)
        out_ref[rows, :] = new
        if not last:
            low_ref[rows, :] = new.astype(bf16)


def update(wires, total, current, place, ratios=None):
    edges, scen = current.shape
    last = ratios is not None
    if last:
        shapes = [jax.ShapeDtypeStruct((edges, scen), f32), jax.ShapeDtypeStruct((CHUNK, scen), f32)]
    else:
        shapes = [pltpu.VMEM((edges, scen), f32), pltpu.VMEM((edges, scen), bf16)]
    return call(
        functools.partial(update_kernel, last),
        shapes,
        [IN_SMEM] + [IN_VMEM] * (7 if last else 6),
        [IN_VMEM] * 2,
        10**7,
    )(place, *wires, total, in_vmem(current), *([ratios] if last else []))


def ring(n, d, stride=1):
    return [(i, (i + d * stride) % n) for i in range(n)]


def swap(bit):
    return [(i, i ^ bit) for i in range(16)]


def sum_ring(value, axis):
    two, one, three = (lax.ppermute(value, axis, ring(4, d)) for d in (2, 1, 3))
    return sum_four([value, one, two, three])


def sum_four(parts):
    zero, one, two, three = parts
    return (zero + two) + (one + three)


def body(coverage, block_mask, edge_prior, test_cost):
    at = lax.axis_index("col")
    x, z, core = at // 4, (at // 2) % 2, at % 2
    place = jnp.stack([x, core, lax.axis_index("row"), z]).astype(jnp.int32)
    for iteration in range(ITERS):
        first = iteration == 0
        pack, unpack = (pack_sums, unpack_sums) if first else (pack_int16, unpack_int16)
        with jax.named_scope("scores"):
            if first:
                away, here, kept, low_weights = first_scores(coverage, block_mask, edge_prior, place)
                current = low_weights
            else:
                away = later_scores(1, kept, low_weights)
                here = later_scores(0, kept, low_weights)
            here = here + lax.ppermute(away, "col", swap(1))
            here = here.reshape(4, -1, here.shape[-1])
        with jax.named_scope("sum_x"):
            parts = [unpack(lax.ppermute(pack(here[d]), "col", ring(16, d, 4))) for d in (1, 2, 3)]
            scores = sum_four([here[0]] + parts)
        if first:
            with jax.named_scope("flip"):
                flipped_here, flipped_away, cost = flip(kept, test_cost, place, scores)
        with jax.named_scope("sum_z"):
            scores = scores + unpack(lax.ppermute(pack(scores), "col", swap(2)))
            ratios = scores[:PAIR] / cost
            low_ratios = ratios.astype(bf16)
            if first:
                sums = [part.astype(bf16) for part in bf16_parts(scores[PAIR:])]
                low_ratios = jnp.concatenate([low_ratios] + sums, axis=0)
        with jax.named_scope("gather"):
            lows = [low_ratios] + [lax.ppermute(low_ratios, "col", ring(16, d, 4)) for d in (1, 2, 3)]
            low_here = jnp.concatenate(lows, axis=0)
            low_away = lax.ppermute(low_here, "col", swap(1))
            if first:
                sums_here, sums_away = low_here, low_away
        with jax.named_scope("total"):
            total = total_load(sums_here, sums_away, low_here, low_away)
            total = float16_parts(total)
        with jax.named_scope("loads"):
            half, size = loads(half_loads_kernel, flipped_here, low_here)
            load, power = loads(whole_loads_kernel, flipped_away, low_away, half, size)
        with jax.named_scope("sum_y"):
            share = load.shape[0] // 4
            parts = [(load[:share], power, from_parts(*total))]
            for d in (1, 2, 3):
                wire = pack_part(load[d * share : (d + 1) * share], power, total)
                parts.append(unpack_part(lax.ppermute(wire, "row", ring(4, d))))
            part, powers, totals = zip(*parts, strict=True)
            power = jnp.maximum(jnp.maximum(powers[0], powers[1]), jnp.maximum(powers[2], powers[3])) + 2.0
        with jax.named_scope("gather_y"):
            wire = pack_load(sum_four(part), power)
            sent = wire.astype(jnp.float16)
            wires = [wire] + [lax.ppermute(sent, "row", ring(4, -d)).astype(f32) for d in (1, 2, 3)]
        with jax.named_scope("total"):
            total = sum_ring(sum_four(totals), "depth")
        with jax.named_scope("update"):
            if iteration < ITERS - 1:
                current, low_weights = update(wires, total, current, place)
            else:
                current, primal = update(wires, total, current, place, ratios)
    return (current, primal)


def solution(mesh):
    placed = (P("row", "col"), P("row", "col"), P("col", "depth"), P("row", "depth"))
    return jax.shard_map(
        body,
        mesh=mesh,
        in_specs=placed,
        out_specs=(P("col", "depth"), P(("row", "col"), "depth")),
        check_vma=False,
    )
```

```python
import functools

import jax
import jax.numpy as jnp
from jax import lax
from jax.experimental import pallas as pl
from jax.experimental.pallas import tpu as pltpu
from jax.sharding import PartitionSpec as P

EDGES = 16384
SCEN = 512
BLOCK = 128
ITERS = 2
TESTS = 12288
CHUNK = 192
PAIR = 2 * CHUNK
HALF = 4 * PAIR
WITH_SUMS = PAIR + 8
GATHERED = PAIR + 32
VMEM_LIMIT = 16 * 1024 * 1024
IN_VMEM = pl.BlockSpec(memory_space=pltpu.VMEM)
IN_SMEM = pl.BlockSpec(memory_space=pltpu.SMEM)
ANYWHERE = pl.BlockSpec(memory_space=pl.ANY)
IN_HBM = pl.BlockSpec(memory_space=pltpu.HBM)
f32 = jnp.float32
bf16 = jnp.bfloat16


def call(kernel, out_shape, in_specs, out_specs, flops, scratch=()):
    return pl.pallas_call(
        kernel,
        in_specs=in_specs,
        out_specs=out_specs,
        out_shape=out_shape,
        scratch_shapes=list(scratch),
        compiler_params=pltpu.CompilerParams(vmem_limit_bytes=VMEM_LIMIT),
        cost_estimate=pl.CostEstimate(flops=flops, bytes_accessed=flops // 400, transcendentals=0),
    )


def in_vmem(value):
    return pltpu.with_memory_space_constraint(value, pltpu.VMEM)


def in_hbm(value):
    return pltpu.with_memory_space_constraint(value, pltpu.HBM)


def tests_of(kept_ref, d, half, edges=slice(None)):
    tests = kept_ref[half * 4 + d, :, :, edges]
    return tests.reshape(PAIR, tests.shape[-1])


def each(count, step):
    def body(n, carry):
        step(n)
        return carry

    lax.fori_loop(0, count, body, 0)


def rows_at(start, size, unit):
    return pl.ds(pl.multiple_of(start, unit), size)


def scores_and_sums(kept, weights, out_ref, d):
    out_ref[rows_at(d * WITH_SUMS, PAIR, 8), :] = jnp.dot(kept, weights, preferred_element_type=f32)
    ones = jnp.ones((8, kept.shape[1]), bf16)
    sums = lax.dot_general(ones, kept, (((1,), (1,)), ((), ())), preferred_element_type=f32)
    out_ref[rows_at(d * WITH_SUMS + PAIR, 8, 8), :] = jnp.concatenate(
        [sums[:1, j * BLOCK : (j + 1) * BLOCK] for j in range(3)] + [jnp.zeros((5, BLOCK), f32)], axis=0
    )


def first_scores_kernel(place_ref, mask_ref, cover_ref, prior_ref, out_ref, kept_ref, weights_ref, rows_ref, tiles_ref, sems):
    tiles = pltpu.make_async_copy(mask_ref, tiles_ref, sems.at[8])
    tiles.start()
    for half in (1, 0):
        core = 1 - place_ref[1] if half else place_ref[1]
        for d in range(4):
            x = lax.rem(place_ref[0] + d, 4)
            pltpu.make_async_copy(
                cover_ref.at[pl.ds(2 * x, 2), core], kept_ref.at[half * 4 + d], sems.at[half * 4 + d]
            ).start()
        if half:
            weights = pltpu.make_async_copy(prior_ref, weights_ref, sems.at[9])
            weights.start()
    edges = cover_ref.shape[-1]
    tiles.wait()
    column = lax.broadcasted_iota(jnp.int32, (tiles_ref.shape[0], edges), 1) // BLOCK
    spread = column == lax.broadcasted_iota(jnp.int32, column.shape, 0)
    rows_ref[...] = lax.dot_general(
        tiles_ref[...].astype(f32), spread.astype(f32), (((0,), (0,)), ((), ())), preferred_element_type=f32
    )
    weights.wait()
    lines = BLOCK // 2
    groups = CHUNK // lines

    def arrive(half, core, d):
        x = lax.rem(place_ref[0] + d, 4)
        slot = half * 4 + d
        pltpu.make_async_copy(cover_ref.at[pl.ds(2 * x, 2), core], kept_ref.at[slot], sems.at[slot]).wait()

        def mask(group):
            z, j = group // groups, lax.rem(group, groups)
            block_row = ((x * 4 + z * 2 + core) * groups + j) // 2
            entry = jnp.broadcast_to(rows_ref[pl.ds(block_row, 1), :], (16, edges)).astype(bf16)
            entry = jnp.concatenate([entry] * (lines // 16), axis=0)
            at = rows_at(j * lines, lines, lines)
            kept_ref[slot, z, at, :] = kept_ref[slot, z, at, :] * entry

        each(2 * groups, mask)

    def other_core(d):
        arrive(1, 1 - place_ref[1], d)
        scores_and_sums(tests_of(kept_ref, d, 1), weights_ref[...], out_ref, d)

    each(4, other_core)
    each(4, lambda d: arrive(0, place_ref[1], d))


def own_scores_kernel(kept_ref, weights_ref, out_ref):
    each(4, lambda d: scores_and_sums(tests_of(kept_ref, d, 0), weights_ref[...], out_ref, d))


def first_scores(cover, mask, prior, place):
    edges, scen = prior.shape
    away, kept, weights = call(
        first_scores_kernel,
        [
            pltpu.VMEM((4 * WITH_SUMS, scen), f32),
            pltpu.VMEM((8, 2, CHUNK, edges), bf16),
            pltpu.VMEM(prior.shape, bf16),
        ],
        [IN_SMEM, IN_HBM, IN_HBM, IN_HBM],
        [IN_VMEM] * 3,
        2 * HALF * edges * scen,
        [
            pltpu.VMEM((mask.shape[0], edges), f32),
            pltpu.VMEM(mask.shape[::-1], mask.dtype),
            pltpu.SemaphoreType.DMA((10,)),
        ],
    )(place, in_hbm(mask.T), in_hbm(cover.reshape(-1, 2, CHUNK, edges)), in_hbm(prior))
    here = call(
        own_scores_kernel,
        pltpu.VMEM((4 * WITH_SUMS, scen), f32),
        [IN_VMEM, IN_VMEM],
        IN_VMEM,
        2 * HALF * edges * scen,
    )(in_vmem(kept), in_vmem(weights))
    return away, here, kept, weights


def scores_kernel(half, kept_ref, weights_ref, out_ref):
    def step(d):
        out_ref[rows_at(d * PAIR, PAIR, PAIR), :] = jnp.dot(
            tests_of(kept_ref, d, half), weights_ref[...], preferred_element_type=f32
        )

    each(4, step)


def later_scores(half, kept, weights):
    edges, scen = weights.shape
    return call(
        functools.partial(scores_kernel, half),
        pltpu.VMEM((HALF, scen), f32),
        [IN_VMEM, IN_VMEM],
        IN_VMEM,
        2 * HALF * edges * scen,
    )(in_vmem(kept), in_vmem(weights))


def flip_kernel(place_ref, kept_ref, cost_ref, after_ref, own_out, other_out, cost_out, cost_in, sems):
    copies = []
    for z in range(2):
        at = pl.multiple_of((place_ref[0] * 4 + z * 2 + place_ref[1]) * CHUNK, CHUNK)
        copy = pltpu.make_async_copy(
            cost_ref.at[pl.ds(at, CHUNK), :], cost_in.at[pl.ds(z * CHUNK, CHUNK), :], sems.at[z]
        )
        copy.start()
        copies.append(copy)
    share = kept_ref.shape[-1] // 4
    for half, out_ref in enumerate((own_out, other_out)):

        def step(n, half=half, out_ref=out_ref):
            e, d = n // 4, lax.rem(n, 4)
            y = lax.rem(place_ref[2] + e, 4)
            tile = tests_of(kept_ref, lax.rem(4 - d, 4), half, rows_at(y * share, share, share))
            out_ref[rows_at(e * share, share, share), rows_at(d * PAIR, PAIR, BLOCK)] = tile.T

        each(16, step)
    for copy in copies:
        copy.wait()
    cost_out[...] = cost_in[...].astype(f32)


def flip(kept, cost, place, after):
    edges = kept.shape[-1]
    return call(
        flip_kernel,
        [
            pltpu.VMEM((edges, HALF), bf16),
            pltpu.VMEM((edges, HALF), bf16),
            pltpu.VMEM((PAIR, cost.shape[1]), f32),
        ],
        [IN_SMEM, IN_VMEM, IN_HBM, ANYWHERE],
        [IN_VMEM, IN_VMEM, IN_VMEM],
        16 * HALF * edges * 128,
        [pltpu.VMEM((PAIR, cost.shape[1]), cost.dtype), pltpu.SemaphoreType.DMA((2,))],
    )(place, in_vmem(kept), in_hbm(cost), after)


def column_sums(low):
    return jnp.dot(jnp.ones((8, low.shape[0]), bf16), low, preferred_element_type=f32)


def lows_of(low_ref):
    stride = low_ref.shape[0] // 4
    return [low_ref[d * stride : d * stride + PAIR, :] for d in range(4)]


def share_of_loads(flipped_ref, lows, rows):
    load = jnp.dot(flipped_ref[rows, :PAIR], lows[0], preferred_element_type=f32)
    for d in range(1, 4):
        load += jnp.dot(flipped_ref[rows, d * PAIR : (d + 1) * PAIR], lows[d], preferred_element_type=f32)
    return load


def half_loads_kernel(flipped_ref, low_ref, load_ref, size_ref):
    size_ref[...] = sum(column_sums(low) for low in lows_of(low_ref))
    share = load_ref.shape[0] // 4

    def step(e):
        rows = rows_at(e * share, share, share)
        load_ref[rows, :] = share_of_loads(flipped_ref, lows_of(low_ref), rows)

    each(4, step)


def whole_loads_kernel(flipped_ref, low_ref, load_in, size_in, load_ref, power_ref):
    size = size_in[...] + sum(column_sums(low) for low in lows_of(low_ref))
    power = jnp.floor(jnp.log2(jnp.maximum(size, 1e-30)))
    power_ref[...] = power
    scale = jnp.exp2(11.0 - power[:1, :])
    share = load_ref.shape[0] // 4

    def step(e):
        rows = rows_at(e * share, share, share)
        load = load_in[rows, :] + share_of_loads(flipped_ref, lows_of(low_ref), rows)
        load_ref[rows, :] = load * jnp.where(e == 0, 1.0, scale)

    each(4, step)


def loads(kernel, flipped, low, *so_far):
    edges, scen = flipped.shape[0], low.shape[1]
    return call(
        kernel,
        [jax.ShapeDtypeStruct((edges, scen), f32), jax.ShapeDtypeStruct((8, scen), f32)],
        [IN_VMEM] * (2 + len(so_far)),
        [IN_VMEM, IN_VMEM],
        2 * HALF * edges * scen,
    )(in_vmem(flipped), low, *so_far)


def total_kernel(sums_ref, low_ref, out_ref):
    totals = [jnp.zeros((32, BLOCK), f32) for _ in range(3)]
    for d, low in enumerate(lows_of(low_ref)):
        sums = sums_ref[d * GATHERED + PAIR : (d + 1) * GATHERED, :]
        for j in range(3):
            totals[j] += jnp.dot(sums, low[j * BLOCK : (j + 1) * BLOCK], preferred_element_type=f32)
    row = lax.broadcasted_iota(jnp.int32, (32, BLOCK), 0)
    total = jnp.zeros((32, BLOCK), f32)
    for j in range(3):
        total += jnp.where(row % 8 == j, totals[j], 0.0)
    out_ref[...] = jnp.full(out_ref.shape, jnp.sum(total), f32)


def total_load(sums, low):
    return call(
        total_kernel,
        jax.ShapeDtypeStruct((8, low.shape[1]), f32),
        [IN_VMEM] * 2,
        IN_VMEM,
        10**8,
    )(sums, low)


def bf16_parts(sums):
    parts = []
    left = sums
    for _ in range(3):
        part = lax.reduce_precision(left, 8, 7)
        left = left - part
        parts.append(part)
    return parts + [jnp.zeros_like(sums)]


def pack_sums(value):
    return jnp.concatenate([value[:PAIR]] + bf16_parts(value[PAIR:]), axis=0).astype(bf16)


def unpack_sums(value):
    value = value.astype(f32)
    sums = value[PAIR : PAIR + 8] + value[PAIR + 8 : PAIR + 16] + value[PAIR + 16 : PAIR + 24]
    return jnp.concatenate([value[:PAIR], sums], axis=0)


def pack_int16(value):
    top = jnp.max(value, axis=0, keepdims=True)
    power = jnp.ceil(jnp.log2(jnp.maximum(top, 1e-30)))
    code = jnp.round(value * jnp.exp2(16.0 - power)) - 32768.0
    code = jnp.clip(code, -32768.0, 32767.0)
    tile = jnp.broadcast_to(power, (16, value.shape[1]))
    return jnp.concatenate([code, tile], axis=0).astype(jnp.int32).astype(jnp.int16)


def unpack_int16(value):
    value = value.astype(jnp.int32).astype(f32)
    return (value[:-16] + 32768.0) * jnp.exp2(value[-16:-15] - 16.0)


def to_float16(value):
    return lax.reduce_precision(value, 5, 10)


def pack_part(load, power, total):
    return jnp.concatenate([load, power] + total, axis=0).astype(jnp.float16)


def float16_parts(total):
    scale = jnp.floor(jnp.log2(jnp.maximum(total, 1e-30)))
    total = total * jnp.exp2(-scale)
    high = to_float16(total)
    return [scale, high, to_float16((total - high) * 1024.0)]


def from_parts(scale, high, low):
    return (high + low * (1.0 / 1024.0)) * jnp.exp2(scale)


def unpack_part(wire):
    wire = wire.astype(f32)
    share = wire.shape[0] - 32
    power, *total = (wire[at : at + 8] for at in range(share, share + 32, 8))
    return wire[:share] * jnp.exp2(power[:1] - 11.0), power, from_parts(*total)


def pack_load(load, power):
    return to_float16(jnp.concatenate([load * jnp.exp2(11.0 - power[:1]), power, power], axis=0))


def update_kernel(last, place_ref, zero, one, two, three, total_ref, current_ref, *rest):
    share = zero.shape[0] - 16
    mean = total_ref[:1, :] * (1.0 / (EDGES * SCEN)) + 1e-06
    if last:
        ratios_ref, out_ref, primal_ref = rest
        own = ratios_ref[pl.ds(pl.multiple_of(place_ref[3] * CHUNK, CHUNK), CHUNK), :]
        primal_ref[...] = TESTS * own / mean
    else:
        out_ref, low_ref = rest
    for d, wire in enumerate((zero, one, two, three)):
        y = lax.rem(place_ref[2] + d, 4)
        factor = -0.25 * jnp.exp2(wire[share : share + 1, :] - 11.0) / mean
        part = share // 4

        def step(n, wire=wire, y=y, factor=factor):
            rows = rows_at(y * share + n * part, part, part)
            load = wire[rows_at(n * part, part, part), :]
            new = current_ref[rows, :].astype(f32) * jnp.exp(load * factor)
            out_ref[rows, :] = new
            if not last:
                low_ref[rows, :] = new.astype(bf16)

        each(4, step)


def update(wires, total, current, place, ratios=None):
    edges, scen = current.shape
    last = ratios is not None
    if last:
        shapes = [jax.ShapeDtypeStruct((edges, scen), f32), jax.ShapeDtypeStruct((CHUNK, scen), f32)]
    else:
        shapes = [pltpu.VMEM((edges, scen), f32), pltpu.VMEM((edges, scen), bf16)]
    return call(
        functools.partial(update_kernel, last),
        shapes,
        [IN_SMEM] + [IN_VMEM] * (7 if last else 6),
        [IN_VMEM] * 2,
        10**7,
    )(place, *wires, total, in_vmem(current), *([ratios] if last else []))


def ring(n, d, stride=1):
    return [(i, (i + d * stride) % n) for i in range(n)]


def swap(bit):
    return [(i, i ^ bit) for i in range(16)]


def pair_sum(value, axis, bit):
    return value + lax.ppermute(value, axis, [(i, i ^ bit) for i in range(4)])


def sum_four(parts):
    zero, one, two, three = parts
    return (zero + two) + (one + three)


def body(coverage, block_mask, edge_prior, test_cost):
    at = lax.axis_index("col")
    x, z, core = at // 4, (at // 2) % 2, at % 2
    place = jnp.stack([x, core, lax.axis_index("row"), z]).astype(jnp.int32)
    for iteration in range(ITERS):
        first = iteration == 0
        pack, unpack = (pack_sums, unpack_sums) if first else (pack_int16, unpack_int16)
        with jax.named_scope("scores"):
            if first:
                away, here, kept, low_weights = first_scores(coverage, block_mask, edge_prior, place)
                current = low_weights
            else:
                away = later_scores(1, kept, low_weights)
                here = later_scores(0, kept, low_weights)
            here = here + lax.ppermute(away, "col", swap(1))
            here = here.reshape(4, -1, here.shape[-1])
        with jax.named_scope("sum_x"):
            parts = [unpack(lax.ppermute(pack(here[d]), "col", ring(16, d, 4))) for d in (1, 2, 3)]
            scores = sum_four([here[0]] + parts)
        if first:
            with jax.named_scope("flip"):
                flipped_here, flipped_away, cost = flip(kept, test_cost, place, scores)
        with jax.named_scope("sum_z"):
            scores = scores + unpack(lax.ppermute(pack(scores), "col", swap(2)))
            ratios = scores[:PAIR] / cost
            low_ratios = ratios.astype(bf16)
            if first:
                sums = [part.astype(bf16) for part in bf16_parts(scores[PAIR:])]
                low_ratios = jnp.concatenate([low_ratios] + sums, axis=0)
        with jax.named_scope("gather"):
            lows = [low_ratios] + [lax.ppermute(low_ratios, "col", ring(16, d, 4)) for d in (1, 2, 3)]
            low_here = jnp.concatenate(lows, axis=0)
            if first:
                sums_here = low_here
        with jax.named_scope("total"):
            total = float16_parts(pair_sum(total_load(sums_here, low_here), "depth", 2))
        with jax.named_scope("gather"):
            low_away = lax.ppermute(low_here, "col", swap(1))
        with jax.named_scope("loads"):
            half, size = loads(half_loads_kernel, flipped_here, low_here)
            load, power = loads(whole_loads_kernel, flipped_away, low_away, half, size)
        with jax.named_scope("sum_y"):
            share = load.shape[0] // 4
            parts = [(load[:share], power, from_parts(*total))]
            for d in (1, 2, 3):
                wire = pack_part(load[d * share : (d + 1) * share], power, total)
                parts.append(unpack_part(lax.ppermute(wire, "row", ring(4, d))))
            part, powers, totals = zip(*parts, strict=True)
            power = jnp.maximum(jnp.maximum(powers[0], powers[1]), jnp.maximum(powers[2], powers[3])) + 2.0
        with jax.named_scope("gather_y"):
            wire = pack_load(sum_four(part), power)
            sent = wire.astype(jnp.float16)
            wires = [wire] + [lax.ppermute(sent, "row", ring(4, -d)).astype(f32) for d in (1, 2, 3)]
        with jax.named_scope("total"):
            total = sum_four(totals)
            total = total + lax.ppermute(total, "col", swap(1))
            total = pair_sum(total, "depth", 1)
        with jax.named_scope("update"):
            if iteration < ITERS - 1:
                current, low_weights = update(wires, total, current, place)
            else:
                current, primal = update(wires, total, current, place, ratios)
    return (current, primal)


def solution(mesh):
    placed = (P("row", "col"), P("row", "col"), P("col", "depth"), P("row", "depth"))
    return jax.shard_map(
        body,
        mesh=mesh,
        in_specs=placed,
        out_specs=(P("col", "depth"), P(("row", "col"), "depth")),
        check_vma=False,
    )
```

```python
import functools

import jax
import jax.numpy as jnp
from jax import lax
from jax.experimental import pallas as pl
from jax.experimental.pallas import tpu as pltpu
from jax.sharding import PartitionSpec as P

EDGES = 16384
SCEN = 512
BLOCK = 128
ITERS = 2
TESTS = 12288
CHUNK = 192
PAIR = 2 * CHUNK
HALF = 4 * PAIR
WITH_SUMS = PAIR + 8
GATHERED = PAIR + 32
VMEM_LIMIT = 16 * 1024 * 1024
IN_VMEM = pl.BlockSpec(memory_space=pltpu.VMEM)
IN_SMEM = pl.BlockSpec(memory_space=pltpu.SMEM)
ANYWHERE = pl.BlockSpec(memory_space=pl.ANY)
IN_HBM = pl.BlockSpec(memory_space=pltpu.HBM)
f32 = jnp.float32
bf16 = jnp.bfloat16


def call(kernel, out_shape, in_specs, out_specs, flops, scratch=()):
    return pl.pallas_call(
        kernel,
        in_specs=in_specs,
        out_specs=out_specs,
        out_shape=out_shape,
        scratch_shapes=list(scratch),
        compiler_params=pltpu.CompilerParams(vmem_limit_bytes=VMEM_LIMIT),
        cost_estimate=pl.CostEstimate(flops=flops, bytes_accessed=flops // 400, transcendentals=0),
    )


def in_vmem(value):
    return pltpu.with_memory_space_constraint(value, pltpu.VMEM)


def in_hbm(value):
    return pltpu.with_memory_space_constraint(value, pltpu.HBM)


def tests_of(kept_ref, d, half, edges=slice(None)):
    tests = kept_ref[half * 4 + d, :, :, edges]
    return tests.reshape(PAIR, tests.shape[-1])


def scores_and_sums(kept, weights, out_ref, d):
    at = d * WITH_SUMS
    out_ref[at : at + PAIR, :] = jnp.dot(kept, weights, preferred_element_type=f32)
    ones = jnp.ones((8, kept.shape[1]), bf16)
    sums = lax.dot_general(ones, kept, (((1,), (1,)), ((), ())), preferred_element_type=f32)
    out_ref[at + PAIR : at + WITH_SUMS, :] = jnp.concatenate(
        [sums[:1, j * BLOCK : (j + 1) * BLOCK] for j in range(3)] + [jnp.zeros((5, BLOCK), f32)], axis=0
    )


def first_scores_kernel(place_ref, mask_ref, cover_ref, prior_ref, out_ref, kept_ref, weights_ref, rows_ref, tiles_ref, sems):
    tiles = pltpu.make_async_copy(mask_ref, tiles_ref, sems.at[8])
    tiles.start()
    copies = {}
    for half in (1, 0):
        core = 1 - place_ref[1] if half else place_ref[1]
        for d in range(4):
            x = lax.rem(place_ref[0] + d, 4)
            copy = pltpu.make_async_copy(
                cover_ref.at[pl.ds(2 * x, 2), core], kept_ref.at[half * 4 + d], sems.at[half * 4 + d]
            )
            copy.start()
            copies[half, d] = copy
        if half:
            weights = pltpu.make_async_copy(prior_ref, weights_ref, sems.at[9])
            weights.start()
    edges = cover_ref.shape[-1]
    tiles.wait()
    column = lax.broadcasted_iota(jnp.int32, (tiles_ref.shape[0], edges), 1) // BLOCK
    spread = column == lax.broadcasted_iota(jnp.int32, column.shape, 0)
    rows_ref[...] = lax.dot_general(
        tiles_ref[...].astype(f32), spread.astype(f32), (((0,), (0,)), ((), ())), preferred_element_type=f32
    )
    weights.wait()
    lines = BLOCK // 2
    for half in (1, 0):
        core = 1 - place_ref[1] if half else place_ref[1]
        for d in range(4):
            copies[half, d].wait()
            for z in range(2):
                chunk = lax.rem(place_ref[0] + d, 4) * 4 + z * 2 + core
                for j in range(CHUNK // lines):
                    block_row = (chunk * (CHUNK // lines) + j) // 2
                    entry = jnp.broadcast_to(rows_ref[pl.ds(block_row, 1), :], (16, edges)).astype(bf16)
                    for k in range(lines // 16):
                        at = slice(j * lines + k * 16, j * lines + k * 16 + 16)
                        kept_ref[half * 4 + d, z, at, :] = kept_ref[half * 4 + d, z, at, :] * entry
            if half:
                scores_and_sums(tests_of(kept_ref, d, half), weights_ref[...], out_ref, d)


def own_scores_kernel(kept_ref, weights_ref, out_ref):
    for d in range(4):
        scores_and_sums(tests_of(kept_ref, d, 0), weights_ref[...], out_ref, d)


def first_scores(cover, mask, prior, place):
    edges, scen = prior.shape
    away, kept, weights = call(
        first_scores_kernel,
        [
            pltpu.VMEM((4 * WITH_SUMS, scen), f32),
            pltpu.VMEM((8, 2, CHUNK, edges), bf16),
            pltpu.VMEM(prior.shape, bf16),
        ],
        [IN_SMEM, IN_HBM, IN_HBM, IN_HBM],
        [IN_VMEM] * 3,
        2 * HALF * edges * scen,
        [
            pltpu.VMEM((mask.shape[0], edges), f32),
            pltpu.VMEM(mask.shape[::-1], mask.dtype),
            pltpu.SemaphoreType.DMA((10,)),
        ],
    )(place, in_hbm(mask.T), in_hbm(cover.reshape(-1, 2, CHUNK, edges)), in_hbm(prior))
    here = call(
        own_scores_kernel,
        pltpu.VMEM((4 * WITH_SUMS, scen), f32),
        [IN_VMEM, IN_VMEM],
        IN_VMEM,
        2 * HALF * edges * scen,
    )(in_vmem(kept), in_vmem(weights))
    return away, here, kept, weights


def scores_kernel(half, kept_ref, weights_ref, out_ref):
    for d in range(4):
        out_ref[d * PAIR : (d + 1) * PAIR, :] = jnp.dot(
            tests_of(kept_ref, d, half), weights_ref[...], preferred_element_type=f32
        )


def later_scores(half, kept, weights):
    edges, scen = weights.shape
    return call(
        functools.partial(scores_kernel, half),
        pltpu.VMEM((HALF, scen), f32),
        [IN_VMEM, IN_VMEM],
        IN_VMEM,
        2 * HALF * edges * scen,
    )(in_vmem(kept), in_vmem(weights))


def flip_kernel(place_ref, kept_ref, cost_ref, after_ref, own_out, other_out, cost_out, cost_in, sems):
    copies = []
    for z in range(2):
        at = pl.multiple_of((place_ref[0] * 4 + z * 2 + place_ref[1]) * CHUNK, CHUNK)
        copy = pltpu.make_async_copy(
            cost_ref.at[pl.ds(at, CHUNK), :], cost_in.at[pl.ds(z * CHUNK, CHUNK), :], sems.at[z]
        )
        copy.start()
        copies.append(copy)
    for half, out_ref in enumerate((own_out, other_out)):
        for d in range(4):
            out_ref[:, d * PAIR : (d + 1) * PAIR] = tests_of(kept_ref, (4 - d) % 4, half).T
    for copy in copies:
        copy.wait()
    cost_out[...] = cost_in[...].astype(f32)


def flip(kept, cost, place, after):
    edges = kept.shape[-1]
    return call(
        flip_kernel,
        [
            pltpu.VMEM((edges, HALF), bf16),
            pltpu.VMEM((edges, HALF), bf16),
            pltpu.VMEM((PAIR, cost.shape[1]), f32),
        ],
        [IN_SMEM, IN_VMEM, IN_HBM, ANYWHERE],
        [IN_VMEM, IN_VMEM, IN_VMEM],
        16 * HALF * edges * 128,
        [pltpu.VMEM((PAIR, cost.shape[1]), cost.dtype), pltpu.SemaphoreType.DMA((2,))],
    )(place, in_vmem(kept), in_hbm(cost), after)


def column_sums(low):
    return jnp.dot(jnp.ones((8, low.shape[0]), bf16), low, preferred_element_type=f32)


def add_loads(flipped_ref, low_ref, load, size):
    stride = low_ref.shape[0] // 4
    for d in range(4):
        low = low_ref[d * stride : d * stride + PAIR, :]
        load += jnp.dot(flipped_ref[:, d * PAIR : (d + 1) * PAIR], low, preferred_element_type=f32)
        size += column_sums(low)
    return load, size


def half_loads_kernel(flipped_ref, low_ref, load_ref, size_ref):
    load, size = add_loads(flipped_ref, low_ref, jnp.zeros(load_ref.shape, f32), jnp.zeros(size_ref.shape, f32))
    load_ref[...] = load
    size_ref[...] = size


def whole_loads_kernel(flipped_ref, low_ref, load_in, size_in, wire_ref):
    load, size = add_loads(flipped_ref, low_ref, load_in[...], size_in[...])
    power = jnp.floor(jnp.log2(jnp.maximum(size, 1e-30)))
    edges = load.shape[0]
    wire_ref[:edges, :] = load * jnp.exp2(11.0 - power[:1, :])
    wire_ref[edges:, :] = jnp.concatenate([power, power], axis=0)


def half_loads(flipped, low):
    edges, scen = flipped.shape[0], low.shape[1]
    return call(
        half_loads_kernel,
        [jax.ShapeDtypeStruct((edges, scen), f32), jax.ShapeDtypeStruct((8, scen), f32)],
        [IN_VMEM] * 2,
        [IN_VMEM, IN_VMEM],
        2 * HALF * edges * scen,
    )(in_vmem(flipped), low)


def whole_loads(flipped, low, load, size):
    edges, scen = load.shape
    return call(
        whole_loads_kernel,
        jax.ShapeDtypeStruct((edges + 16, scen), f32),
        [IN_VMEM] * 4,
        IN_VMEM,
        2 * HALF * edges * scen,
    )(in_vmem(flipped), low, load, size)


def total_kernel(sums_own, sums_away, low_own, low_away, out_ref):
    totals = [jnp.zeros((32, BLOCK), f32) for _ in range(3)]
    stride = low_own.shape[0] // 4
    for sums_ref, low_ref in ((sums_own, low_own), (sums_away, low_away)):
        for d in range(4):
            sums = sums_ref[d * GATHERED + PAIR : (d + 1) * GATHERED, :]
            for j in range(3):
                low = low_ref[d * stride + j * BLOCK : d * stride + (j + 1) * BLOCK, :]
                totals[j] += jnp.dot(sums, low, preferred_element_type=f32)
    row = lax.broadcasted_iota(jnp.int32, (32, BLOCK), 0)
    total = jnp.zeros((32, BLOCK), f32)
    for j in range(3):
        total += jnp.where(row % 8 == j, totals[j], 0.0)
    out_ref[...] = jnp.full(out_ref.shape, jnp.sum(total), f32)


def total_load(sums_own, sums_away, low_own, low_away):
    return call(
        total_kernel,
        jax.ShapeDtypeStruct((8, low_own.shape[1]), f32),
        [IN_VMEM] * 4,
        IN_VMEM,
        10**8,
    )(sums_own, sums_away, low_own, low_away)


def bf16_parts(sums):
    parts = []
    left = sums
    for _ in range(3):
        part = lax.reduce_precision(left, 8, 7)
        left = left - part
        parts.append(part)
    return parts + [jnp.zeros_like(sums)]


def pack_sums(value):
    return jnp.concatenate([value[:PAIR]] + bf16_parts(value[PAIR:]), axis=0).astype(bf16)


def unpack_sums(value):
    value = value.astype(f32)
    sums = value[PAIR : PAIR + 8] + value[PAIR + 8 : PAIR + 16] + value[PAIR + 16 : PAIR + 24]
    return jnp.concatenate([value[:PAIR], sums], axis=0)


def pack_int16(value):
    top = jnp.max(value, axis=0, keepdims=True)
    power = jnp.ceil(jnp.log2(jnp.maximum(top, 1e-30)))
    code = jnp.round(value * jnp.exp2(16.0 - power)) - 32768.0
    code = jnp.clip(code, -32768.0, 32767.0)
    tile = jnp.broadcast_to(power, (16, value.shape[1]))
    return jnp.concatenate([code, tile], axis=0).astype(jnp.int32).astype(jnp.int16)


def unpack_int16(value):
    value = value.astype(jnp.int32).astype(f32)
    return (value[:-16] + 32768.0) * jnp.exp2(value[-16:-15] - 16.0)


def to_float16(value):
    return lax.reduce_precision(value, 5, 10)


def update_kernel(last, place_ref, zero, one, two, three, total_ref, current_ref, *rest):
    edges = current_ref.shape[0]
    mean = total_ref[:1, :] * (1.0 / (EDGES * SCEN)) + 1e-06
    if last:
        ratios_ref, out_ref, primal_ref = rest
        own = ratios_ref[pl.ds(pl.multiple_of(place_ref[3] * CHUNK, CHUNK), CHUNK), :]
        primal_ref[...] = TESTS * own / mean
    else:
        out_ref, low_ref = rest
    wires = (zero, one, two, three)
    factors = [-0.25 * jnp.exp2(wire[edges : edges + 1, :] - 11.0) / mean for wire in wires]
    part = 128
    for n in range(edges // part):
        rows = slice(n * part, (n + 1) * part)
        loads = [wire[rows, :] * factor for wire, factor in zip(wires, factors, strict=True)]
        new = current_ref[rows, :].astype(f32) * jnp.exp((loads[0] + loads[2]) + (loads[1] + loads[3]))
        out_ref[rows, :] = new
        if not last:
            low_ref[rows, :] = new.astype(bf16)


def update(wires, total, current, place, ratios=None):
    edges, scen = current.shape
    last = ratios is not None
    if last:
        shapes = [jax.ShapeDtypeStruct((edges, scen), f32), jax.ShapeDtypeStruct((CHUNK, scen), f32)]
    else:
        shapes = [pltpu.VMEM((edges, scen), f32), pltpu.VMEM((edges, scen), bf16)]
    return call(
        functools.partial(update_kernel, last),
        shapes,
        [IN_SMEM] + [IN_VMEM] * (7 if last else 6),
        [IN_VMEM] * 2,
        10**7,
    )(place, *wires, total, in_vmem(current), *([ratios] if last else []))


def ring(n, d, stride=1):
    return [(i, (i + d * stride) % n) for i in range(n)]


def swap(bit):
    return [(i, i ^ bit) for i in range(16)]


def pair_sum(value, axis, bit):
    return value + lax.ppermute(value, axis, [(i, i ^ bit) for i in range(4)])


def sum_four(parts):
    zero, one, two, three = parts
    return (zero + two) + (one + three)


def body(coverage, block_mask, edge_prior, test_cost):
    at = lax.axis_index("col")
    x, z, core = at // 4, (at // 2) % 2, at % 2
    place = jnp.stack([x, core, lax.axis_index("row"), z]).astype(jnp.int32)
    for iteration in range(ITERS):
        first = iteration == 0
        pack, unpack = (pack_sums, unpack_sums) if first else (pack_int16, unpack_int16)
        with jax.named_scope("scores"):
            if first:
                away, here, kept, low_weights = first_scores(coverage, block_mask, edge_prior, place)
                current = low_weights
            else:
                away = later_scores(1, kept, low_weights)
                here = later_scores(0, kept, low_weights)
            here = here + lax.ppermute(away, "col", swap(1))
            here = here.reshape(4, -1, here.shape[-1])
        with jax.named_scope("sum_x"):
            parts = [unpack(lax.ppermute(pack(here[d]), "col", ring(16, d, 4))) for d in (1, 2, 3)]
            scores = sum_four([here[0]] + parts)
        if first:
            with jax.named_scope("flip"):
                flipped_here, flipped_away, cost = flip(kept, test_cost, place, scores)
        with jax.named_scope("sum_z"):
            scores = scores + unpack(lax.ppermute(pack(scores), "col", swap(2)))
            ratios = scores[:PAIR] / cost
            low_ratios = ratios.astype(bf16)
            if first:
                sums = [part.astype(bf16) for part in bf16_parts(scores[PAIR:])]
                low_ratios = jnp.concatenate([low_ratios] + sums, axis=0)
        with jax.named_scope("gather"):
            lows = [low_ratios] + [lax.ppermute(low_ratios, "col", ring(16, d, 4)) for d in (1, 2, 3)]
            low_here = jnp.concatenate(lows, axis=0)
            low_away = lax.ppermute(low_here, "col", swap(1))
            if first:
                sums_here, sums_away = low_here, low_away
        with jax.named_scope("total"):
            total = total_load(sums_here, sums_away, low_here, low_away)
            total = sum_four([total] + [lax.ppermute(total, "row", ring(4, d)) for d in (1, 2, 3)])
            row_total = total
            total = pair_sum(pair_sum(total, "depth", 1), "depth", 2)
        with jax.named_scope("loads"):
            load, size = half_loads(flipped_here, low_here)
            load = whole_loads(flipped_away, low_away, load, size)
            load = to_float16(jnp.concatenate([load[:-8], jnp.minimum(row_total, 1.0)], axis=0))
        with jax.named_scope("sum_y"):
            sent = load.astype(jnp.float16)
            wires = [load] + [lax.ppermute(sent, "row", ring(4, d)).astype(f32) for d in (1, 2, 3)]
        with jax.named_scope("update"):
            if iteration < ITERS - 1:
                current, low_weights = update(wires, total, current, place)
            else:
                current, primal = update(wires, total, current, place, ratios)
    return (current, primal)


def solution(mesh):
    placed = (P("row", "col"), P("row", "col"), P("col", "depth"), P("row", "depth"))
    return jax.shard_map(
        body,
        mesh=mesh,
        in_specs=placed,
        out_specs=(P("col", "depth"), P(("row", "col"), "depth")),
        check_vma=False,
    )
```

```python
import functools

import jax
import jax.numpy as jnp
from jax import lax
from jax.experimental import pallas as pl
from jax.experimental.pallas import tpu as pltpu
from jax.sharding import PartitionSpec as P

EDGES = 16384
SCEN = 512
BLOCK = 128
ITERS = 2
TESTS = 12288
CHUNK = 192
PAIR = 2 * CHUNK
HALF = 4 * PAIR
WITH_SUMS = PAIR + 8
GATHERED = PAIR + 32
VMEM_LIMIT = 16 * 1024 * 1024
IN_VMEM = pl.BlockSpec(memory_space=pltpu.VMEM)
IN_SMEM = pl.BlockSpec(memory_space=pltpu.SMEM)
ANYWHERE = pl.BlockSpec(memory_space=pl.ANY)
IN_HBM = pl.BlockSpec(memory_space=pltpu.HBM)
f32 = jnp.float32
bf16 = jnp.bfloat16


def call(kernel, out_shape, in_specs, out_specs, flops, scratch=()):
    return pl.pallas_call(
        kernel,
        in_specs=in_specs,
        out_specs=out_specs,
        out_shape=out_shape,
        scratch_shapes=list(scratch),
        compiler_params=pltpu.CompilerParams(vmem_limit_bytes=VMEM_LIMIT),
        cost_estimate=pl.CostEstimate(flops=flops, bytes_accessed=flops // 400, transcendentals=0),
    )


def in_vmem(value):
    return pltpu.with_memory_space_constraint(value, pltpu.VMEM)


def in_hbm(value):
    return pltpu.with_memory_space_constraint(value, pltpu.HBM)


def tests_of(kept_ref, d, half, edges=slice(None)):
    tests = kept_ref[half * 4 + d, :, :, edges]
    return tests.reshape(PAIR, tests.shape[-1])


def scores_and_sums(kept, weights, out_ref, d):
    at = d * WITH_SUMS
    out_ref[at : at + PAIR, :] = jnp.dot(kept, weights, preferred_element_type=f32)
    ones = jnp.ones((8, kept.shape[1]), bf16)
    sums = lax.dot_general(ones, kept, (((1,), (1,)), ((), ())), preferred_element_type=f32)
    out_ref[at + PAIR : at + WITH_SUMS, :] = jnp.concatenate(
        [sums[:1, j * BLOCK : (j + 1) * BLOCK] for j in range(3)] + [jnp.zeros((5, BLOCK), f32)], axis=0
    )


def first_scores_kernel(place_ref, mask_ref, cover_ref, prior_ref, out_ref, kept_ref, weights_ref, rows_ref, tiles_ref, sems):
    tiles = pltpu.make_async_copy(mask_ref, tiles_ref, sems.at[8])
    tiles.start()
    for half in (1, 0):
        core = 1 - place_ref[1] if half else place_ref[1]
        for d in range(4):
            x = lax.rem(place_ref[0] + d, 4)
            pltpu.make_async_copy(
                cover_ref.at[pl.ds(2 * x, 2), core], kept_ref.at[half * 4 + d], sems.at[half * 4 + d]
            ).start()
        if half:
            weights = pltpu.make_async_copy(prior_ref, weights_ref, sems.at[9])
            weights.start()
    edges = cover_ref.shape[-1]
    tiles.wait()
    column = lax.broadcasted_iota(jnp.int32, (tiles_ref.shape[0], edges), 1) // BLOCK
    spread = column == lax.broadcasted_iota(jnp.int32, column.shape, 0)
    rows_ref[...] = lax.dot_general(
        tiles_ref[...].astype(f32), spread.astype(f32), (((0,), (0,)), ((), ())), preferred_element_type=f32
    )
    weights.wait()
    lines = BLOCK // 2

    def arrive(half, core, d):
        x = lax.rem(place_ref[0] + d, 4)
        slot = half * 4 + d
        pltpu.make_async_copy(cover_ref.at[pl.ds(2 * x, 2), core], kept_ref.at[slot], sems.at[slot]).wait()
        for z in range(2):
            for j in range(CHUNK // lines):
                block_row = ((x * 4 + z * 2 + core) * (CHUNK // lines) + j) // 2
                entry = jnp.broadcast_to(rows_ref[pl.ds(block_row, 1), :], (16, edges)).astype(bf16)
                for k in range(lines // 16):
                    at = slice(j * lines + k * 16, j * lines + k * 16 + 16)
                    kept_ref[slot, z, at, :] = kept_ref[slot, z, at, :] * entry

    for d in range(4):
        arrive(1, 1 - place_ref[1], d)
        scores_and_sums(tests_of(kept_ref, d, 1), weights_ref[...], out_ref, d)

    def own(d, carry):
        arrive(0, place_ref[1], d)
        return carry

    lax.fori_loop(0, 4, own, 0)


def own_scores_kernel(kept_ref, weights_ref, out_ref):
    for d in range(4):
        scores_and_sums(tests_of(kept_ref, d, 0), weights_ref[...], out_ref, d)


def first_scores(cover, mask, prior, place):
    edges, scen = prior.shape
    away, kept, weights = call(
        first_scores_kernel,
        [
            pltpu.VMEM((4 * WITH_SUMS, scen), f32),
            pltpu.VMEM((8, 2, CHUNK, edges), bf16),
            pltpu.VMEM(prior.shape, bf16),
        ],
        [IN_SMEM, IN_HBM, IN_HBM, IN_HBM],
        [IN_VMEM] * 3,
        2 * HALF * edges * scen,
        [
            pltpu.VMEM((mask.shape[0], edges), f32),
            pltpu.VMEM(mask.shape[::-1], mask.dtype),
            pltpu.SemaphoreType.DMA((10,)),
        ],
    )(place, in_hbm(mask.T), in_hbm(cover.reshape(-1, 2, CHUNK, edges)), in_hbm(prior))
    here = call(
        own_scores_kernel,
        pltpu.VMEM((4 * WITH_SUMS, scen), f32),
        [IN_VMEM, IN_VMEM],
        IN_VMEM,
        2 * HALF * edges * scen,
    )(in_vmem(kept), in_vmem(weights))
    return away, here, kept, weights


def scores_kernel(half, kept_ref, weights_ref, out_ref):
    for d in range(4):
        out_ref[d * PAIR : (d + 1) * PAIR, :] = jnp.dot(
            tests_of(kept_ref, d, half), weights_ref[...], preferred_element_type=f32
        )


def later_scores(half, kept, weights):
    edges, scen = weights.shape
    return call(
        functools.partial(scores_kernel, half),
        pltpu.VMEM((HALF, scen), f32),
        [IN_VMEM, IN_VMEM],
        IN_VMEM,
        2 * HALF * edges * scen,
    )(in_vmem(kept), in_vmem(weights))


def flip_kernel(place_ref, kept_ref, cost_ref, after_ref, own_out, other_out, cost_out, cost_in, sems):
    copies = []
    for z in range(2):
        at = pl.multiple_of((place_ref[0] * 4 + z * 2 + place_ref[1]) * CHUNK, CHUNK)
        copy = pltpu.make_async_copy(
            cost_ref.at[pl.ds(at, CHUNK), :], cost_in.at[pl.ds(z * CHUNK, CHUNK), :], sems.at[z]
        )
        copy.start()
        copies.append(copy)
    for half, out_ref in enumerate((own_out, other_out)):

        def step(d, carry, half=half, out_ref=out_ref):
            columns = pl.ds(pl.multiple_of(d * PAIR, BLOCK), PAIR)
            out_ref[:, columns] = tests_of(kept_ref, lax.rem(4 - d, 4), half).T
            return carry

        lax.fori_loop(0, 4, step, 0)
    for copy in copies:
        copy.wait()
    cost_out[...] = cost_in[...].astype(f32)


def flip(kept, cost, place, after):
    edges = kept.shape[-1]
    return call(
        flip_kernel,
        [
            pltpu.VMEM((edges, HALF), bf16),
            pltpu.VMEM((edges, HALF), bf16),
            pltpu.VMEM((PAIR, cost.shape[1]), f32),
        ],
        [IN_SMEM, IN_VMEM, IN_HBM, ANYWHERE],
        [IN_VMEM, IN_VMEM, IN_VMEM],
        16 * HALF * edges * 128,
        [pltpu.VMEM((PAIR, cost.shape[1]), cost.dtype), pltpu.SemaphoreType.DMA((2,))],
    )(place, in_vmem(kept), in_hbm(cost), after)


def column_sums(low):
    return jnp.dot(jnp.ones((8, low.shape[0]), bf16), low, preferred_element_type=f32)


def add_loads(flipped_ref, low_ref, load, size):
    stride = low_ref.shape[0] // 4
    for d in range(4):
        low = low_ref[d * stride : d * stride + PAIR, :]
        load += jnp.dot(flipped_ref[:, d * PAIR : (d + 1) * PAIR], low, preferred_element_type=f32)
        size += column_sums(low)
    return load, size


def half_loads_kernel(flipped_ref, low_ref, load_ref, size_ref):
    load, size = add_loads(flipped_ref, low_ref, jnp.zeros(load_ref.shape, f32), jnp.zeros(size_ref.shape, f32))
    load_ref[...] = load
    size_ref[...] = size


def whole_loads_kernel(flipped_ref, low_ref, load_in, size_in, wire_ref):
    load, size = add_loads(flipped_ref, low_ref, load_in[...], size_in[...])
    power = jnp.floor(jnp.log2(jnp.maximum(size, 1e-30)))
    edges = load.shape[0]
    wire_ref[:edges, :] = load * jnp.exp2(11.0 - power[:1, :])
    wire_ref[edges:, :] = jnp.concatenate([power, power], axis=0)


def half_loads(flipped, low):
    edges, scen = flipped.shape[0], low.shape[1]
    return call(
        half_loads_kernel,
        [jax.ShapeDtypeStruct((edges, scen), f32), jax.ShapeDtypeStruct((8, scen), f32)],
        [IN_VMEM] * 2,
        [IN_VMEM, IN_VMEM],
        2 * HALF * edges * scen,
    )(in_vmem(flipped), low)


def whole_loads(flipped, low, load, size):
    edges, scen = load.shape
    return call(
        whole_loads_kernel,
        jax.ShapeDtypeStruct((edges + 16, scen), f32),
        [IN_VMEM] * 4,
        IN_VMEM,
        2 * HALF * edges * scen,
    )(in_vmem(flipped), low, load, size)


def total_kernel(sums_own, sums_away, low_own, low_away, out_ref):
    totals = [jnp.zeros((32, BLOCK), f32) for _ in range(3)]
    stride = low_own.shape[0] // 4
    for sums_ref, low_ref in ((sums_own, low_own), (sums_away, low_away)):
        for d in range(4):
            sums = sums_ref[d * GATHERED + PAIR : (d + 1) * GATHERED, :]
            for j in range(3):
                low = low_ref[d * stride + j * BLOCK : d * stride + (j + 1) * BLOCK, :]
                totals[j] += jnp.dot(sums, low, preferred_element_type=f32)
    row = lax.broadcasted_iota(jnp.int32, (32, BLOCK), 0)
    total = jnp.zeros((32, BLOCK), f32)
    for j in range(3):
        total += jnp.where(row % 8 == j, totals[j], 0.0)
    out_ref[...] = jnp.full(out_ref.shape, jnp.sum(total), f32)


def total_load(sums_own, sums_away, low_own, low_away):
    return call(
        total_kernel,
        jax.ShapeDtypeStruct((8, low_own.shape[1]), f32),
        [IN_VMEM] * 4,
        IN_VMEM,
        10**8,
    )(sums_own, sums_away, low_own, low_away)


def bf16_parts(sums):
    parts = []
    left = sums
    for _ in range(3):
        part = lax.reduce_precision(left, 8, 7)
        left = left - part
        parts.append(part)
    return parts + [jnp.zeros_like(sums)]


def pack_sums(value):
    return jnp.concatenate([value[:PAIR]] + bf16_parts(value[PAIR:]), axis=0).astype(bf16)


def unpack_sums(value):
    value = value.astype(f32)
    sums = value[PAIR : PAIR + 8] + value[PAIR + 8 : PAIR + 16] + value[PAIR + 16 : PAIR + 24]
    return jnp.concatenate([value[:PAIR], sums], axis=0)


def pack_int16(value):
    top = jnp.max(value, axis=0, keepdims=True)
    power = jnp.ceil(jnp.log2(jnp.maximum(top, 1e-30)))
    code = jnp.round(value * jnp.exp2(16.0 - power)) - 32768.0
    code = jnp.clip(code, -32768.0, 32767.0)
    tile = jnp.broadcast_to(power, (16, value.shape[1]))
    return jnp.concatenate([code, tile], axis=0).astype(jnp.int32).astype(jnp.int16)


def unpack_int16(value):
    value = value.astype(jnp.int32).astype(f32)
    return (value[:-16] + 32768.0) * jnp.exp2(value[-16:-15] - 16.0)


def to_float16(value):
    return lax.reduce_precision(value, 5, 10)


def update_kernel(last, place_ref, zero, one, two, three, total_ref, current_ref, *rest):
    edges = current_ref.shape[0]
    mean = total_ref[:1, :] * (1.0 / (EDGES * SCEN)) + 1e-06
    if last:
        ratios_ref, out_ref, primal_ref = rest
        own = ratios_ref[pl.ds(pl.multiple_of(place_ref[3] * CHUNK, CHUNK), CHUNK), :]
        primal_ref[...] = TESTS * own / mean
    else:
        out_ref, low_ref = rest
    wires = (zero, one, two, three)
    factors = [-0.25 * jnp.exp2(wire[edges : edges + 1, :] - 11.0) / mean for wire in wires]
    part = 128
    for n in range(edges // part):
        rows = slice(n * part, (n + 1) * part)
        loads = [wire[rows, :] * factor for wire, factor in zip(wires, factors, strict=True)]
        new = current_ref[rows, :].astype(f32) * jnp.exp((loads[0] + loads[2]) + (loads[1] + loads[3]))
        out_ref[rows, :] = new
        if not last:
            low_ref[rows, :] = new.astype(bf16)


def update(wires, total, current, place, ratios=None):
    edges, scen = current.shape
    last = ratios is not None
    if last:
        shapes = [jax.ShapeDtypeStruct((edges, scen), f32), jax.ShapeDtypeStruct((CHUNK, scen), f32)]
    else:
        shapes = [pltpu.VMEM((edges, scen), f32), pltpu.VMEM((edges, scen), bf16)]
    return call(
        functools.partial(update_kernel, last),
        shapes,
        [IN_SMEM] + [IN_VMEM] * (7 if last else 6),
        [IN_VMEM] * 2,
        10**7,
    )(place, *wires, total, in_vmem(current), *([ratios] if last else []))


def ring(n, d, stride=1):
    return [(i, (i + d * stride) % n) for i in range(n)]


def swap(bit):
    return [(i, i ^ bit) for i in range(16)]


def sum_ring(value, axis):
    return sum_four([value] + [lax.ppermute(value, axis, ring(4, d)) for d in (1, 2, 3)])


def sum_four(parts):
    zero, one, two, three = parts
    return (zero + two) + (one + three)


def body(coverage, block_mask, edge_prior, test_cost):
    at = lax.axis_index("col")
    x, z, core = at // 4, (at // 2) % 2, at % 2
    place = jnp.stack([x, core, lax.axis_index("row"), z]).astype(jnp.int32)
    for iteration in range(ITERS):
        first = iteration == 0
        pack, unpack = (pack_sums, unpack_sums) if first else (pack_int16, unpack_int16)
        with jax.named_scope("scores"):
            if first:
                away, here, kept, low_weights = first_scores(coverage, block_mask, edge_prior, place)
                current = low_weights
            else:
                away = later_scores(1, kept, low_weights)
                here = later_scores(0, kept, low_weights)
            here = here + lax.ppermute(away, "col", swap(1))
            here = here.reshape(4, -1, here.shape[-1])
        with jax.named_scope("sum_x"):
            parts = [unpack(lax.ppermute(pack(here[d]), "col", ring(16, d, 4))) for d in (1, 2, 3)]
            scores = sum_four([here[0]] + parts)
        if first:
            with jax.named_scope("flip"):
                flipped_here, flipped_away, cost = flip(kept, test_cost, place, scores)
        with jax.named_scope("sum_z"):
            scores = scores + unpack(lax.ppermute(pack(scores), "col", swap(2)))
            ratios = scores[:PAIR] / cost
            low_ratios = ratios.astype(bf16)
            if first:
                sums = [part.astype(bf16) for part in bf16_parts(scores[PAIR:])]
                low_ratios = jnp.concatenate([low_ratios] + sums, axis=0)
        with jax.named_scope("gather"):
            lows = [low_ratios] + [lax.ppermute(low_ratios, "col", ring(16, d, 4)) for d in (1, 2, 3)]
            low_here = jnp.concatenate(lows, axis=0)
            low_away = lax.ppermute(low_here, "col", swap(1))
            if first:
                sums_here, sums_away = low_here, low_away
        with jax.named_scope("total"):
            total = total_load(sums_here, sums_away, low_here, low_away)
            total = row_total = sum_ring(total, "row")
            total = sum_ring(total, "depth")
        with jax.named_scope("loads"):
            load, size = half_loads(flipped_here, low_here)
            load = whole_loads(flipped_away, low_away, load, size)
            load = to_float16(jnp.concatenate([load[:-8], jnp.minimum(row_total, 1.0)], axis=0))
        with jax.named_scope("sum_y"):
            sent = load.astype(jnp.float16)
            wires = [load] + [lax.ppermute(sent, "row", ring(4, d)).astype(f32) for d in (1, 2, 3)]
        with jax.named_scope("update"):
            if iteration < ITERS - 1:
                current, low_weights = update(wires, total, current, place)
            else:
                current, primal = update(wires, total, current, place, ratios)
    return (current, primal)


def solution(mesh):
    placed = (P("row", "col"), P("row", "col"), P("col", "depth"), P("row", "depth"))
    return jax.shard_map(
        body,
        mesh=mesh,
        in_specs=placed,
        out_specs=(P("col", "depth"), P(("row", "col"), "depth")),
        check_vma=False,
    )
```

```python
import functools

import jax
import jax.numpy as jnp
from jax import lax
from jax.experimental import pallas as pl
from jax.experimental.pallas import tpu as pltpu
from jax.sharding import PartitionSpec as P

EDGES = 16384
SCEN = 512
BLOCK = 128
ITERS = 2
TESTS = 12288
CHUNK = 192
PAIR = 2 * CHUNK
HALF = 4 * PAIR
WITH_SUMS = PAIR + 8
GATHERED = PAIR + 32
VMEM_LIMIT = 16 * 1024 * 1024
IN_VMEM = pl.BlockSpec(memory_space=pltpu.VMEM)
IN_SMEM = pl.BlockSpec(memory_space=pltpu.SMEM)
ANYWHERE = pl.BlockSpec(memory_space=pl.ANY)
IN_HBM = pl.BlockSpec(memory_space=pltpu.HBM)
f32 = jnp.float32
bf16 = jnp.bfloat16


def call(kernel, out_shape, in_specs, out_specs, flops, scratch=()):
    return pl.pallas_call(
        kernel,
        in_specs=in_specs,
        out_specs=out_specs,
        out_shape=out_shape,
        scratch_shapes=list(scratch),
        compiler_params=pltpu.CompilerParams(vmem_limit_bytes=VMEM_LIMIT),
        cost_estimate=pl.CostEstimate(flops=flops, bytes_accessed=flops // 400, transcendentals=0),
    )


def in_vmem(value):
    return pltpu.with_memory_space_constraint(value, pltpu.VMEM)


def in_hbm(value):
    return pltpu.with_memory_space_constraint(value, pltpu.HBM)


def tests_of(kept_ref, d, half, edges=slice(None)):
    tests = kept_ref[half * 4 + d, :, :, edges]
    return tests.reshape(PAIR, tests.shape[-1])


def scores_and_sums(kept, weights, out_ref, d):
    at = pl.multiple_of(d * WITH_SUMS, 8)
    out_ref[pl.ds(at, PAIR), :] = jnp.dot(kept, weights, preferred_element_type=f32)
    ones = jnp.ones((8, kept.shape[1]), bf16)
    sums = lax.dot_general(ones, kept, (((1,), (1,)), ((), ())), preferred_element_type=f32)
    out_ref[pl.ds(at + PAIR, 8), :] = jnp.concatenate(
        [sums[:1, j * BLOCK : (j + 1) * BLOCK] for j in range(3)] + [jnp.zeros((5, BLOCK), f32)], axis=0
    )


def first_scores_kernel(place_ref, mask_ref, cover_ref, prior_ref, out_ref, kept_ref, weights_ref, rows_ref, tiles_ref, sems):
    tiles = pltpu.make_async_copy(mask_ref, tiles_ref, sems.at[8])
    tiles.start()
    for half in (1, 0):
        core = 1 - place_ref[1] if half else place_ref[1]
        for d in range(4):
            x = lax.rem(place_ref[0] + d, 4)
            pltpu.make_async_copy(
                cover_ref.at[pl.ds(2 * x, 2), core], kept_ref.at[half * 4 + d], sems.at[half * 4 + d]
            ).start()
        if half:
            weights = pltpu.make_async_copy(prior_ref, weights_ref, sems.at[9])
            weights.start()
    edges = cover_ref.shape[-1]
    tiles.wait()
    column = lax.broadcasted_iota(jnp.int32, (tiles_ref.shape[0], edges), 1) // BLOCK
    spread = column == lax.broadcasted_iota(jnp.int32, column.shape, 0)
    rows_ref[...] = lax.dot_general(
        tiles_ref[...].astype(f32), spread.astype(f32), (((0,), (0,)), ((), ())), preferred_element_type=f32
    )
    weights.wait()
    lines = BLOCK // 2

    def arrive(half, core, d):
        x = lax.rem(place_ref[0] + d, 4)
        slot = half * 4 + d
        pltpu.make_async_copy(cover_ref.at[pl.ds(2 * x, 2), core], kept_ref.at[slot], sems.at[slot]).wait()
        for z in range(2):
            for j in range(CHUNK // lines):
                block_row = ((x * 4 + z * 2 + core) * (CHUNK // lines) + j) // 2
                entry = jnp.broadcast_to(rows_ref[pl.ds(block_row, 1), :], (16, edges)).astype(bf16)
                for k in range(lines // 16):
                    at = slice(j * lines + k * 16, j * lines + k * 16 + 16)
                    kept_ref[slot, z, at, :] = kept_ref[slot, z, at, :] * entry

    for d in range(4):
        arrive(1, 1 - place_ref[1], d)
        scores_and_sums(tests_of(kept_ref, d, 1), weights_ref[...], out_ref, d)

    def own(d, carry):
        arrive(0, place_ref[1], d)
        return carry

    lax.fori_loop(0, 4, own, 0)


def own_scores_kernel(kept_ref, weights_ref, out_ref):
    def step(d, carry):
        scores_and_sums(tests_of(kept_ref, d, 0), weights_ref[...], out_ref, d)
        return carry

    lax.fori_loop(0, 4, step, 0)


def first_scores(cover, mask, prior, place):
    edges, scen = prior.shape
    away, kept, weights = call(
        first_scores_kernel,
        [
            pltpu.VMEM((4 * WITH_SUMS, scen), f32),
            pltpu.VMEM((8, 2, CHUNK, edges), bf16),
            pltpu.VMEM(prior.shape, bf16),
        ],
        [IN_SMEM, IN_HBM, IN_HBM, IN_HBM],
        [IN_VMEM] * 3,
        2 * HALF * edges * scen,
        [
            pltpu.VMEM((mask.shape[0], edges), f32),
            pltpu.VMEM(mask.shape[::-1], mask.dtype),
            pltpu.SemaphoreType.DMA((10,)),
        ],
    )(place, in_hbm(mask.T), in_hbm(cover.reshape(-1, 2, CHUNK, edges)), in_hbm(prior))
    here = call(
        own_scores_kernel,
        pltpu.VMEM((4 * WITH_SUMS, scen), f32),
        [IN_VMEM, IN_VMEM],
        IN_VMEM,
        2 * HALF * edges * scen,
    )(in_vmem(kept), in_vmem(weights))
    return away, here, kept, weights


def scores_kernel(half, kept_ref, weights_ref, out_ref):
    for d in range(4):
        out_ref[d * PAIR : (d + 1) * PAIR, :] = jnp.dot(
            tests_of(kept_ref, d, half), weights_ref[...], preferred_element_type=f32
        )


def later_scores(half, kept, weights):
    edges, scen = weights.shape
    return call(
        functools.partial(scores_kernel, half),
        pltpu.VMEM((HALF, scen), f32),
        [IN_VMEM, IN_VMEM],
        IN_VMEM,
        2 * HALF * edges * scen,
    )(in_vmem(kept), in_vmem(weights))


def flip_kernel(place_ref, kept_ref, cost_ref, after_ref, own_out, other_out, cost_out, cost_in, sems):
    copies = []
    for z in range(2):
        at = pl.multiple_of((place_ref[0] * 4 + z * 2 + place_ref[1]) * CHUNK, CHUNK)
        copy = pltpu.make_async_copy(
            cost_ref.at[pl.ds(at, CHUNK), :], cost_in.at[pl.ds(z * CHUNK, CHUNK), :], sems.at[z]
        )
        copy.start()
        copies.append(copy)
    for half, out_ref in enumerate((own_out, other_out)):

        def step(d, carry, half=half, out_ref=out_ref):
            columns = pl.ds(pl.multiple_of(d * PAIR, BLOCK), PAIR)
            out_ref[:, columns] = tests_of(kept_ref, lax.rem(4 - d, 4), half).T
            return carry

        lax.fori_loop(0, 4, step, 0)
    for copy in copies:
        copy.wait()
    cost_out[...] = cost_in[...].astype(f32)


def flip(kept, cost, place, after):
    edges = kept.shape[-1]
    return call(
        flip_kernel,
        [
            pltpu.VMEM((edges, HALF), bf16),
            pltpu.VMEM((edges, HALF), bf16),
            pltpu.VMEM((PAIR, cost.shape[1]), f32),
        ],
        [IN_SMEM, IN_VMEM, IN_HBM, ANYWHERE],
        [IN_VMEM, IN_VMEM, IN_VMEM],
        16 * HALF * edges * 128,
        [pltpu.VMEM((PAIR, cost.shape[1]), cost.dtype), pltpu.SemaphoreType.DMA((2,))],
    )(place, in_vmem(kept), in_hbm(cost), after)


def column_sums(low):
    return jnp.dot(jnp.ones((8, low.shape[0]), bf16), low, preferred_element_type=f32)


def add_loads(flipped_ref, low_ref, load, size):
    stride = low_ref.shape[0] // 4
    for d in range(4):
        low = low_ref[d * stride : d * stride + PAIR, :]
        load += jnp.dot(flipped_ref[:, d * PAIR : (d + 1) * PAIR], low, preferred_element_type=f32)
        size += column_sums(low)
    return load, size


def half_loads_kernel(flipped_ref, low_ref, load_ref, size_ref):
    load, size = add_loads(flipped_ref, low_ref, jnp.zeros(load_ref.shape, f32), jnp.zeros(size_ref.shape, f32))
    load_ref[...] = load
    size_ref[...] = size


def whole_loads_kernel(flipped_ref, low_ref, load_in, size_in, wire_ref):
    load, size = add_loads(flipped_ref, low_ref, load_in[...], size_in[...])
    power = jnp.floor(jnp.log2(jnp.maximum(size, 1e-30)))
    edges = load.shape[0]
    wire_ref[:edges, :] = load * jnp.exp2(11.0 - power[:1, :])
    wire_ref[edges:, :] = jnp.concatenate([power, power], axis=0)


def half_loads(flipped, low):
    edges, scen = flipped.shape[0], low.shape[1]
    return call(
        half_loads_kernel,
        [jax.ShapeDtypeStruct((edges, scen), f32), jax.ShapeDtypeStruct((8, scen), f32)],
        [IN_VMEM] * 2,
        [IN_VMEM, IN_VMEM],
        2 * HALF * edges * scen,
    )(in_vmem(flipped), low)


def whole_loads(flipped, low, load, size):
    edges, scen = load.shape
    return call(
        whole_loads_kernel,
        jax.ShapeDtypeStruct((edges + 16, scen), f32),
        [IN_VMEM] * 4,
        IN_VMEM,
        2 * HALF * edges * scen,
    )(in_vmem(flipped), low, load, size)


def total_kernel(sums_ref, low_ref, out_ref):
    totals = [jnp.zeros((32, BLOCK), f32) for _ in range(3)]
    stride = low_ref.shape[0] // 4
    for d in range(4):
        sums = sums_ref[d * GATHERED + PAIR : (d + 1) * GATHERED, :]
        for j in range(3):
            low = low_ref[d * stride + j * BLOCK : d * stride + (j + 1) * BLOCK, :]
            totals[j] += jnp.dot(sums, low, preferred_element_type=f32)
    row = lax.broadcasted_iota(jnp.int32, (32, BLOCK), 0)
    total = jnp.zeros((32, BLOCK), f32)
    for j in range(3):
        total += jnp.where(row % 8 == j, totals[j], 0.0)
    out_ref[...] = jnp.full(out_ref.shape, jnp.sum(total), f32)


def total_load(sums, low):
    return call(
        total_kernel,
        jax.ShapeDtypeStruct((8, low.shape[1]), f32),
        [IN_VMEM] * 2,
        IN_VMEM,
        10**8,
    )(sums, low)


def bf16_parts(sums):
    parts = []
    left = sums
    for _ in range(3):
        part = lax.reduce_precision(left, 8, 7)
        left = left - part
        parts.append(part)
    return parts + [jnp.zeros_like(sums)]


def pack_sums(value):
    return jnp.concatenate([value[:PAIR]] + bf16_parts(value[PAIR:]), axis=0).astype(bf16)


def unpack_sums(value):
    value = value.astype(f32)
    sums = value[PAIR : PAIR + 8] + value[PAIR + 8 : PAIR + 16] + value[PAIR + 16 : PAIR + 24]
    return jnp.concatenate([value[:PAIR], sums], axis=0)


def pack_int16(value):
    top = jnp.max(value, axis=0, keepdims=True)
    power = jnp.ceil(jnp.log2(jnp.maximum(top, 1e-30)))
    code = jnp.round(value * jnp.exp2(16.0 - power)) - 32768.0
    code = jnp.clip(code, -32768.0, 32767.0)
    tile = jnp.broadcast_to(power, (16, value.shape[1]))
    return jnp.concatenate([code, tile], axis=0).astype(jnp.int32).astype(jnp.int16)


def unpack_int16(value):
    value = value.astype(jnp.int32).astype(f32)
    return (value[:-16] + 32768.0) * jnp.exp2(value[-16:-15] - 16.0)


def to_float16(value):
    return lax.reduce_precision(value, 5, 10)


def update_kernel(last, place_ref, zero, one, two, three, total_ref, current_ref, *rest):
    edges = current_ref.shape[0]
    mean = total_ref[:1, :] * (1.0 / (EDGES * SCEN)) + 1e-06
    if last:
        ratios_ref, out_ref, primal_ref = rest
        own = ratios_ref[pl.ds(pl.multiple_of(place_ref[3] * CHUNK, CHUNK), CHUNK), :]
        primal_ref[...] = TESTS * own / mean
    else:
        out_ref, low_ref = rest
    wires = (zero, one, two, three)
    factors = [-0.25 * jnp.exp2(wire[edges : edges + 1, :] - 11.0) / mean for wire in wires]
    part = 256

    def step(n, carry):
        rows = pl.ds(pl.multiple_of(n * part, part), part)
        loads = [wire[rows, :] * factor for wire, factor in zip(wires, factors, strict=True)]
        new = current_ref[rows, :].astype(f32) * jnp.exp((loads[0] + loads[2]) + (loads[1] + loads[3]))
        out_ref[rows, :] = new
        if not last:
            low_ref[rows, :] = new.astype(bf16)
        return carry

    lax.fori_loop(0, edges // part, step, 0)


def update(wires, total, current, place, ratios=None):
    edges, scen = current.shape
    last = ratios is not None
    if last:
        shapes = [jax.ShapeDtypeStruct((edges, scen), f32), jax.ShapeDtypeStruct((CHUNK, scen), f32)]
    else:
        shapes = [pltpu.VMEM((edges, scen), f32), pltpu.VMEM((edges, scen), bf16)]
    return call(
        functools.partial(update_kernel, last),
        shapes,
        [IN_SMEM] + [IN_VMEM] * (7 if last else 6),
        [IN_VMEM] * 2,
        10**7,
    )(place, *wires, total, in_vmem(current), *([ratios] if last else []))


def ring(n, d, stride=1):
    return [(i, (i + d * stride) % n) for i in range(n)]


def swap(bit):
    return [(i, i ^ bit) for i in range(16)]


def sum_ring(value, axis):
    return sum_four([value] + [lax.ppermute(value, axis, ring(4, d)) for d in (1, 2, 3)])


def sum_four(parts):
    zero, one, two, three = parts
    return (zero + two) + (one + three)


def body(coverage, block_mask, edge_prior, test_cost):
    at = lax.axis_index("col")
    x, z, core = at // 4, (at // 2) % 2, at % 2
    place = jnp.stack([x, core, lax.axis_index("row"), z]).astype(jnp.int32)
    for iteration in range(ITERS):
        first = iteration == 0
        pack, unpack = (pack_sums, unpack_sums) if first else (pack_int16, unpack_int16)
        with jax.named_scope("scores"):
            if first:
                away, here, kept, low_weights = first_scores(coverage, block_mask, edge_prior, place)
                current = low_weights
            else:
                away = later_scores(1, kept, low_weights)
                here = later_scores(0, kept, low_weights)
            here = here + lax.ppermute(away, "col", swap(1))
            here = here.reshape(4, -1, here.shape[-1])
        with jax.named_scope("sum_x"):
            parts = [unpack(lax.ppermute(pack(here[d]), "col", ring(16, d, 4))) for d in (1, 2, 3)]
            scores = sum_four([here[0]] + parts)
        if first:
            with jax.named_scope("flip"):
                flipped_here, flipped_away, cost = flip(kept, test_cost, place, scores)
        with jax.named_scope("sum_z"):
            scores = scores + unpack(lax.ppermute(pack(scores), "col", swap(2)))
            ratios = scores[:PAIR] / cost
            low_ratios = ratios.astype(bf16)
            if first:
                sums = [part.astype(bf16) for part in bf16_parts(scores[PAIR:])]
                low_ratios = jnp.concatenate([low_ratios] + sums, axis=0)
        with jax.named_scope("gather"):
            lows = [low_ratios] + [lax.ppermute(low_ratios, "col", ring(16, d, 4)) for d in (1, 2, 3)]
            low_here = jnp.concatenate(lows, axis=0)
            low_away = lax.ppermute(low_here, "col", swap(1))
            if first:
                sums_here = low_here
        with jax.named_scope("total"):
            total = total_load(sums_here, low_here)
            total = row_total = sum_ring(total, "row")
            total = total + lax.ppermute(total, "col", swap(1))
            total = sum_ring(total, "depth")
        with jax.named_scope("loads"):
            load, size = half_loads(flipped_here, low_here)
            load = whole_loads(flipped_away, low_away, load, size)
            load = to_float16(jnp.concatenate([load[:-8], jnp.minimum(row_total, 1.0)], axis=0))
        with jax.named_scope("sum_y"):
            sent = load.astype(jnp.float16)
            wires = [load] + [lax.ppermute(sent, "row", ring(4, d)).astype(f32) for d in (1, 2, 3)]
        with jax.named_scope("update"):
            if iteration < ITERS - 1:
                current, low_weights = update(wires, total, current, place)
            else:
                current, primal = update(wires, total, current, place, ratios)
    return (current, primal)


def solution(mesh):
    placed = (P("row", "col"), P("row", "col"), P("col", "depth"), P("row", "depth"))
    return jax.shard_map(
        body,
        mesh=mesh,
        in_specs=placed,
        out_specs=(P("col", "depth"), P(("row", "col"), "depth")),
        check_vma=False,
    )
```
